256 devices in a mesh: section: 2 (over core), rep: 32 (over z, x), tp: 4 (over y).
Axes of the slice: x: 4, y: 4, z: 8, core: 2. Of those that a mesh axis runs over, the one named last changes fastest.
Arguments:
- inputs: bfloat16 [1, 32, 128, 2560], P(None, 'rep', None, 'tp'), may hold values from -50 to 50
- weights: bfloat16 [2, 2560, 2560], P('section', None, 'tp'), may hold values from -0.125 to 0.125
- wiring: int32 [1, 1, 32], replicated, may hold values from 0 to 31, as said below
- lengths: int32 [1, 32], replicated, may hold values from 1 to 128, 3072 in all within a row
- targets: bfloat16 [1, 32, 128, 2560], P(None, 'rep', None, 'tp'), may hold values from -6 to 6
Outputs:
- acts: bfloat16 [2, 1, 32, 2, 128, 2560], P('section', None, 'rep', None, None, 'tp')
- grad_w: float32 [2, 2560, 2560], P('section', 'rep', 'tp')
The draws below stay inside these ranges and needn't reach their ends.
Inputs may be any that keep to these rules, and one draw needn't show every extreme that they name: wiring[s - 1, w, j] is the replica of segment s that holds micro-batch j of wave w. In every segment and wave no replica holds more than 2 micro-batches and some replica holds exactly 2. Two micro-batches of one wave that share a replica at segment s - 1 never share a replica at segment s.
All inputs are finite; a program needn't handle non-finite values.
Results may differ from the reference program's by a relative error of at most 0.019.
Values may be sent and summed in bfloat16 or wider, within the bound.
No kernel may reach another device: no remote copies, remote signals or barrier semaphores. Data moves between devices by JAX's collectives and lax.ppermute only.
A program may use at most 64 MiB of HBM per device.

```python
import math
import jax
import jax.numpy as jnp
import numpy as np
from jax import lax

D = 2560
TOK = 128
WAVES = 1
WCAP = 2
N_SECTION = 2
N_REP = 32


def draw_inputs(key, part):
    key = jax.random.fold_in(key, 5)
    base_key, row_key, col_key = jax.random.split(key, 3)
    base_draw = jnp.clip(jax.random.normal(base_key, (WAVES, N_REP, TOK, D), jnp.float32), -5.0, 5.0)
    row_scale = jnp.exp(jax.random.uniform(row_key, (WAVES, N_REP, TOK, 1), jnp.float32, 0.0, 2.3))
    col_scale = jnp.exp(jax.random.uniform(col_key, (D,), jnp.float32, 0.0, 2.3))
    return (base_draw * row_scale * col_scale * 0.1).astype(jnp.bfloat16)


def draw_wiring(key, part):
    key = jax.random.fold_in(key, 11)
    sources = [jnp.arange(N_REP, dtype=jnp.int32) for wave_id in range(WAVES)]
    segment_rows = []
    for segment_id in range(N_SECTION - 1):
        wave_rows = []
        for wave_id in range(WAVES):
            sub_key = jax.random.fold_in(key, segment_id * WAVES + wave_id)
            perm_key, pick_key, score_key = jax.random.split(sub_key, 3)
            shuffled = jax.random.permutation(perm_key, N_REP).astype(jnp.int32)
            anchor = sources[wave_id]
            moved_one = jax.random.randint(pick_key, (), 0, N_REP)
            scores = jax.random.randint(score_key, (N_REP,), 0, 1 << 20) * N_REP + jnp.arange(N_REP, dtype=jnp.int32)
            allowed = anchor != anchor[moved_one]
            partner = jnp.argmax(jnp.where(allowed, scores, -1))
            target_rows = shuffled.at[moved_one].set(shuffled[partner])
            wave_rows.append(target_rows)
            sources[wave_id] = target_rows
        segment_rows.append(jnp.stack(wave_rows))
    return jnp.stack(segment_rows).astype(jnp.int32)


def block_scale(rng, extent, pieces, smallest, largest):
    def one(position, blocks):
        heights = jax.random.uniform(jax.random.fold_in(jax.random.fold_in(rng, 6), position), (blocks,), jnp.float32, smallest / len(pieces), largest / len(pieces))
        return jnp.repeat(jnp.exp(heights), extent[position] // blocks).reshape((-1,) + (1,) * (len(extent) - position - 1))

    factor_of = one(*pieces[0])
    for cut in pieces[1:]:
        factor_of = factor_of * one(*cut)
    return factor_of


def split_up(amount, total, bound, skew):
    portions = [(1 << 20) // math.isqrt(standing ** skew) + 1 for standing in range(2, amount + 1)]
    surplus, counts = total - bound - (amount - 1), [1] * (amount - 1)
    while surplus > 0:
        movable = [i for i in range(amount - 1) if counts[i] < bound]
        pool, budget = sum([portions[i] for i in movable]), surplus
        for i in movable:
            addition = min(bound - counts[i], max(1, budget * portions[i] // pool), surplus)
            counts[i] = counts[i] + addition
            surplus = surplus - addition
    return np.array([bound] + counts)


def ragged(rng, number_of, total, reach, slope):
    if number_of == 2:
        one = jax.random.randint(rng, (), max(1, total - reach), min(reach, total - 1) + 1)
        return jnp.stack([one, total - one])
    sizes = jnp.asarray(split_up(number_of, total, reach, slope), jnp.int32)
    twos = (number_of - 1) // 2
    source_of, taker = sizes[1:1 + 2 * twos:2], sizes[2:2 + 2 * twos:2]
    margin = jnp.minimum(source_of - 1, reach - taker)
    shifted = jax.random.randint(jax.random.fold_in(rng, 1), (twos,), 0, 1 << 20) % (margin + 1)
    sizes = sizes.at[1:1 + 2 * twos:2].set(source_of - shifted).at[2:2 + 2 * twos:2].set(taker + shifted)
    return sizes[jax.random.permutation(jax.random.fold_in(rng, 2), number_of)]


def centred(stream_key, dims, spread, bound, cuts=(), kind=jnp.bfloat16):
    factor_of = block_scale(stream_key, dims, cuts, -0.22, 0.18) if cuts else 1.0
    drawn = jax.random.normal(stream_key, dims, jnp.float32) * spread * factor_of
    return jnp.minimum(jnp.maximum(drawn, -bound), bound).astype(kind)


def setup_inputs(seed: int = 0) -> dict:
    keys = jax.random.split(jax.random.key(seed), 6)
    return {
        "inputs": draw_inputs(jax.random.fold_in(keys[5], 71), 0),
        "weights": centred(keys[1], (N_SECTION, D, D), D ** -0.5, 0.125, ((0, 2), (2, 4))),
        "wiring": draw_wiring(jax.random.fold_in(keys[5], 71), 0),
        "lengths": jax.vmap(lambda own: ragged(own, N_REP, N_REP * TOK * 3 // 4, TOK, 1))(jax.random.split(keys[3], WAVES)).reshape((WAVES, N_REP)).astype(jnp.int32),
        "targets": centred(keys[4], (WAVES, N_REP, TOK, D), 1.0, 6.0, ((1, 32), (3, 4))),
    }


epsilon = 1e-06
root_half = 0.7071067811865476
normal_peak = 0.3989422804014327

def gelu_value(mixed_now):
    return 0.5 * mixed_now * (1.0 + lax.erf(mixed_now * root_half))

def gelu_slope(mixed_now):
    return 0.5 * (1.0 + lax.erf(mixed_now * root_half)) + mixed_now * jnp.exp(-0.5 * mixed_now * mixed_now) * normal_peak

def holder_tables(wiring, wave_count, replicas):
    first_row = jnp.broadcast_to(jnp.arange(replicas, dtype=jnp.int32)[None, None, :], (1, wave_count, replicas))
    holder = jnp.concatenate([first_row, wiring.astype(jnp.int32)], axis=0)
    same_rep = holder[..., :, None] == holder[..., None, :]
    earlier = jnp.arange(replicas)[None, :] < jnp.arange(replicas)[:, None]
    slot_of = lax.optimization_barrier(jnp.sum(jnp.where(same_rep & earlier, 1, 0), axis=-1)).astype(jnp.int32)
    return (holder, slot_of)

def replica_sum(normed_slots, delta_slots, feat_width):
    replicas = normed_slots.shape[1]

    def add_one(rep_index, running):
        left_rows = lax.dynamic_index_in_dim(normed_slots, rep_index, 1, keepdims=False).reshape(-1, feat_width)
        right_rows = lax.dynamic_index_in_dim(delta_slots, rep_index, 1, keepdims=False).reshape(-1, feat_width)
        part_sum = jnp.dot(left_rows.T, right_rows, preferred_element_type=jnp.float32).astype(jnp.bfloat16)
        part_sum = lax.optimization_barrier(part_sum)
        return running + part_sum.astype(jnp.float32)
    return lax.fori_loop(0, replicas, add_one, jnp.zeros((feat_width, feat_width), jnp.float32))

def reference(inputs, weights, wiring, lengths, targets):
    wave_count, replicas, tokens, feat_width = inputs.shape
    segment_count = weights.shape[0]
    holder, slot_of = holder_tables(wiring, wave_count, replicas)
    to_rep = (holder[..., None] == jnp.arange(replicas, dtype=jnp.int32)).astype(jnp.float32)
    to_slot = (slot_of[..., None] == jnp.arange(WCAP, dtype=jnp.int32)).astype(jnp.float32)
    placer = jnp.einsum('swjr,swjc->swjrc', to_rep, to_slot)

    def slotted(values, segment_id):
        return jnp.einsum('wjrc,wjtd->wrctd', placer[segment_id], values.astype(jnp.float32))
    current = inputs
    saved_list = []
    layers = []
    for segment_id in range(segment_count):
        wide_now = current.astype(jnp.float32)
        row_scale = lax.rsqrt(lax.optimization_barrier(jnp.mean(wide_now * wide_now, axis=-1, keepdims=True)) + epsilon)
        normed = (wide_now * row_scale).astype(jnp.bfloat16)
        mixed_now = jnp.dot(normed.reshape(-1, feat_width), weights[segment_id], preferred_element_type=jnp.float32).reshape(wide_now.shape)
        output = (wide_now + gelu_value(mixed_now)).astype(jnp.bfloat16)
        saved_list.append((wide_now, row_scale, normed, mixed_now))
        layers.append(slotted(output, segment_id).astype(jnp.bfloat16))
        current = output
    acts = jnp.stack(layers)
    valid_mask = (jnp.arange(tokens)[None, None, :] < lengths[:, :, None]).astype(jnp.float32)
    factor = 1.0 / math.sqrt(wave_count * replicas * tokens)
    grad_now = ((current.astype(jnp.float32) - targets.astype(jnp.float32)) * valid_mask[..., None] * factor).astype(jnp.bfloat16)
    grad_list = [None] * segment_count
    for segment_id in reversed(range(segment_count)):
        wide_now, row_scale, normed, mixed_now = saved_list[segment_id]
        delta_now = (grad_now.astype(jnp.float32) * gelu_slope(mixed_now)).astype(jnp.bfloat16)
        grad_list[segment_id] = replica_sum(slotted(normed, segment_id).astype(jnp.bfloat16), slotted(delta_now, segment_id).astype(jnp.bfloat16), feat_width)
        back_sum = jnp.dot(delta_now.reshape(-1, feat_width), weights[segment_id].T, preferred_element_type=jnp.float32).reshape(wide_now.shape)
        stat_sum = lax.optimization_barrier(jnp.sum(mixed_now * delta_now.astype(jnp.float32), axis=-1, keepdims=True)) / feat_width
        grad_now = (grad_now.astype(jnp.float32) + row_scale * (back_sum - wide_now * row_scale * stat_sum)).astype(jnp.bfloat16)
    return (acts, jnp.stack(grad_list))
```

```python
import functools
import math

import jax
import jax.numpy as jnp
from jax import lax
from jax.experimental import pallas as pl
from jax.experimental.pallas import tpu as pltpu
from jax.sharding import PartitionSpec as P

WCAP = 2
EPS = 1e-06
ROOT_HALF = 0.7071067811865476
NORMAL_PEAK = 0.3989422804014327
VMEM_LIMIT = 24 * 1024 * 1024
VM = pl.BlockSpec(memory_space=pltpu.VMEM)
SM = pl.BlockSpec(memory_space=pltpu.SMEM)
ANY = pl.BlockSpec(memory_space=pl.ANY)
BF = jnp.bfloat16
F32 = jnp.float32


def gelu_value(v):
    return 0.5 * v * (1.0 + lax.erf(v * ROOT_HALF))


def gelu_slope(v):
    return 0.5 * (1.0 + lax.erf(v * ROOT_HALF)) + v * jnp.exp(-0.5 * v * v) * NORMAL_PEAK


def call(body, out_shape, in_specs, name, scratch=(), flops=0, nbytes=0):
    many = isinstance(out_shape, (tuple, list))
    return pl.pallas_call(
        body,
        out_shape=out_shape,
        in_specs=in_specs,
        out_specs=tuple(VM for _ in out_shape) if many else VM,
        scratch_shapes=scratch,
        name=name,
        compiler_params=pltpu.CompilerParams(vmem_limit_bytes=VMEM_LIMIT),
        cost_estimate=pl.CostEstimate(flops=flops, bytes_accessed=nbytes, transcendentals=0),
    )


def rows_scale(blocks, feat):
    total = None
    for block in blocks:
        wide = block.astype(F32)
        part = jnp.sum(wide * wide, axis=-1, keepdims=True)
        total = part if total is None else total + part
    return lax.rsqrt(total / feat + EPS)


def rows_product(refs, w_ref, tp_pos, tp_count):
    width = refs[0].shape[-1]
    total = None
    for k, ref in enumerate(refs):
        start = pl.multiple_of(lax.rem(tp_pos + tp_count - k, tp_count) * width, width)
        part = jnp.dot(ref[...], w_ref[pl.ds(start, width), :], preferred_element_type=F32)
        total = part if total is None else total + part
    return total


def first_kernel(tp_count, feat, info, *refs):
    blocks, (w_ref, x1_ref, mixed_ref, scale_ref) = refs[:tp_count], refs[tp_count:]

    @pl.when(info[0] == 0)
    def _():
        scale = rows_scale([b[...] for b in blocks], feat)
        mixed = rows_product(blocks, w_ref, info[2], tp_count) * scale
        x1_ref[...] = (blocks[0][...].astype(F32) + gelu_value(mixed)).astype(BF)
        mixed_ref[...] = mixed
        scale_ref[...] = jnp.broadcast_to(scale, scale_ref.shape)


def second_kernel(tp_count, feat, loss_scale, info, lengths, *refs):
    blocks = refs[:tp_count]
    w_ref, goal_ref, x2_ref, delta_ref = refs[tp_count : tp_count + 4]
    back_refs = refs[tp_count + 4 :]

    @pl.when(info[0] == 1)
    def _():
        tp_pos = info[2]
        tokens, width = blocks[0].shape
        scale = rows_scale([b[...] for b in blocks], feat)
        mixed = rows_product(blocks, w_ref, tp_pos, tp_count) * scale
        x2 = (blocks[0][...].astype(F32) + gelu_value(mixed)).astype(BF)
        x2_ref[...] = x2
        token_ids = lax.broadcasted_iota(jnp.int32, (tokens, 1), 0)
        valid = jnp.where(token_ids < lengths[0, info[1]], loss_scale, 0.0)
        grad = ((x2.astype(F32) - goal_ref[...].astype(F32)) * valid).astype(BF)
        delta = (grad.astype(F32) * gelu_slope(mixed)).astype(BF)
        wide_delta = delta.astype(F32)
        stat = jnp.sum(mixed * wide_delta, axis=-1, keepdims=True) / feat
        delta_ref[...] = (wide_delta * scale).astype(BF)
        for k in range(tp_count):
            start = pl.multiple_of(lax.rem(tp_pos + tp_count - k, tp_count) * width, width)
            back = lax.dot_general(
                delta,
                w_ref[pl.ds(start, width), :],
                (((1,), (1,)), ((), ())),
                preferred_element_type=F32,
            )
            row = scale * (back - blocks[k][...].astype(F32) * (scale * stat))
            if k == 0:
                row = row + grad.astype(F32)
            back_refs[k][...] = row.astype(BF)


def turn_kernel(tp_count, x_count, z_count, info, *refs):
    first = refs[:tp_count]
    second = refs[tp_count : 2 * tp_count]
    mixed_ref, scale_ref, _ = refs[2 * tp_count : 2 * tp_count + 3]
    outs = refs[2 * tp_count + 3 : 2 * tp_count + 3 + x_count]
    slope_ref, turned = refs[2 * tp_count + 3 + x_count :]
    tp_pos = info[2]
    x_pos = lax.rem(info[1], x_count)
    rows = turned.shape[2]

    def put(blocks):
        for k in range(tp_count):
            source = lax.rem(tp_pos + tp_count - k, tp_count)
            flipped = blocks[k][...].T
            per = flipped.shape[0] // rows
            for i in range(per):
                place = source * (per // x_count) + i // x_count
                turned[i % x_count, place] = flipped[i * rows : (i + 1) * rows]

    @pl.when(info[0] == 0)
    def _():
        put(first)
        slope_ref[...] = gelu_slope(mixed_ref[...]) * scale_ref[:, :1]

    @pl.when(info[0] == 1)
    def _():
        put(second)

    for k in range(x_count):
        outs[k][...] = turned[lax.rem(x_pos + k, x_count)].reshape(outs[k].shape)


def delta_kernel(tp_count, info, *refs):
    back, (slope_ref, other_ref, out_ref) = refs[:tp_count], refs[tp_count:]

    @pl.when(info[0] == 0)
    def _():
        grad = back[0][...].astype(F32)
        for ref in back[1:]:
            grad = grad + ref[...].astype(F32)
        grad = grad.astype(BF).astype(F32)
        out_ref[...] = (grad * slope_ref[...]).astype(BF)

    @pl.when(info[0] != 0)
    def _():
        out_ref[...] = other_ref[...]


def part_kernel(x_count, z_count, info, *refs):
    turned, deltas = refs[:x_count], refs[x_count : 2 * x_count]
    outs = refs[2 * x_count : 2 * x_count + z_count]
    parts = refs[-1]
    left = jnp.concatenate([t[...] for t in turned], axis=1)
    right = jnp.concatenate([d[...] for d in deltas], axis=0)
    part = jnp.dot(left, right, preferred_element_type=F32).astype(BF)
    parts[...] = part.reshape(parts.shape)
    z_pos = info[1] // x_count
    for k in range(z_count):
        outs[k][...] = parts[lax.rem(z_pos + k, z_count)]


def sum_kernel(*refs):
    total = refs[0][...].astype(F32)
    for ref in refs[1:-1]:
        total = total + ref[...].astype(F32)
    refs[-1][...] = total


def make_table(wiring, table, counts, replicas):
    @pl.loop(0, replicas)
    def _(r):
        counts[r] = 0
        for c in range(WCAP):
            table[r * WCAP + c] = -1

    @pl.loop(0, replicas)
    def _(j):
        r = wiring[0, 0, j]
        table[r * WCAP + counts[r]] = j
        counts[r] = counts[r] + 1


def route_kernel(x_count, z_count, info, wiring, *refs):
    items = refs[:z_count]
    outs = refs[z_count : z_count + x_count]
    table, counts = refs[z_count + x_count :]

    @pl.when(info[0] == 1)
    def _():
        make_table(wiring, table, counts, x_count * z_count)
        x_pos = lax.rem(info[1], x_count)
        z_pos = info[1] // x_count
        for k in range(x_count):
            target = z_pos * x_count + lax.rem(x_pos + k, x_count)
            for c in range(WCAP):
                j = table[target * WCAP + c]
                here = (j >= 0) & (lax.rem(j, x_count) == x_pos)
                steps = lax.rem(z_pos + z_count - j // x_count, z_count)
                for m in range(z_count):

                    @pl.when(here & (steps == m))
                    def _(k=k, c=c, m=m):
                        outs[k][c] = items[m][...]


def place_kernel(x_count, z_count, info, wiring, x1_ref, *refs):
    slots = refs[:x_count]
    out_ref, table, counts = refs[x_count:]

    @pl.when(info[0] == 0)
    def _():
        out_ref[0] = x1_ref[...]
        for c in range(1, WCAP):
            out_ref[c] = jnp.zeros_like(x1_ref)

    @pl.when(info[0] == 1)
    def _():
        make_table(wiring, table, counts, x_count * z_count)
        x_pos = lax.rem(info[1], x_count)
        for c in range(WCAP):
            j = table[info[1] * WCAP + c]

            @pl.when(j < 0)
            def _(c=c):
                out_ref[c] = jnp.zeros_like(x1_ref)

            steps = lax.rem(x_pos + x_count - lax.rem(j, x_count), x_count)
            for k in range(x_count):

                @pl.when((j >= 0) & (steps == k))
                def _(c=c, k=k):
                    out_ref[c] = slots[k][c]


def on_device(x_count, z_count, inputs, weights, wiring, lengths, targets):
    replicas = lax.axis_size("rep")
    tp_count = lax.axis_size("tp")
    section = lax.axis_index("section")
    rep = lax.axis_index("rep")
    tp = lax.axis_index("tp")
    info = jnp.stack([section, rep, tp]).astype(jnp.int32)
    _, _, tokens, width = inputs.shape
    weight = weights[0]
    feat = weight.shape[0]
    x0 = inputs.reshape(tokens, width)
    goal = targets.reshape(tokens, width)
    rows = feat // replicas
    loss_scale = 1.0 / math.sqrt(replicas * tokens)
    like = jax.ShapeDtypeStruct((tokens, width), BF)
    wide = jax.ShapeDtypeStruct((tokens, width), F32)

    def tp_move(value, k, source, target):
        pairs = [
            (source * tp_count + y, target * tp_count + (y + k) % tp_count)
            for y in range(tp_count)
        ]
        return lax.ppermute(value, ("section", "tp"), pairs)

    def x_pairs(k):
        return [
            (z * x_count + x, z * x_count + (x + k) % x_count)
            for z in range(z_count)
            for x in range(x_count)
        ]

    def z_pairs(k):
        return [
            (z * x_count + x, ((z + k) % z_count) * x_count + x)
            for z in range(z_count)
            for x in range(x_count)
        ]

    def rep_move(value, pairs):
        return lax.ppermute(value, "rep", pairs)

    def rep_move_last(value, pairs):
        pairs = [(replicas + a, replicas + b) for a, b in pairs]
        return lax.ppermute(value, ("section", "rep"), pairs)

    flops = 2 * tokens * feat * width
    first_blocks = [x0] + [tp_move(x0, k, 0, 0) for k in range(1, tp_count)]
    x1, mixed, scale = call(
        functools.partial(first_kernel, tp_count, feat),
        (like, wide, jax.ShapeDtypeStruct((tokens, 128), F32)),
        [SM] + [VM] * (tp_count + 1),
        "first",
        flops=flops,
        nbytes=2 * feat * width,
    )(info, *first_blocks, weight)
    second_blocks = [tp_move(x1, k, 0, 1) for k in range(tp_count)]
    x2, delta1, *back = call(
        functools.partial(second_kernel, tp_count, feat, loss_scale),
        (like,) * (2 + tp_count),
        [SM, SM] + [VM] * (tp_count + 2),
        "second",
        flops=2 * flops,
        nbytes=2 * feat * width,
    )(info, lengths, *second_blocks, weight, goal)
    back_blocks = [tp_move(back[k], (tp_count - k) % tp_count, 1, 0) for k in range(tp_count)]
    flat = jax.ShapeDtypeStruct((feat // x_count, tokens), BF)
    *turned, slope = call(
        functools.partial(turn_kernel, tp_count, x_count, z_count),
        (flat,) * x_count + (wide,),
        [SM] + [VM] * (2 * tp_count + 2) + [ANY],
        "turn",
        scratch=[pltpu.VMEM((x_count, z_count, rows, tokens), BF)],
        flops=flops // 8,
        nbytes=2 * feat * tokens,
    )(info, *first_blocks, *second_blocks, mixed, scale, delta1)
    lefts = [turned[0]] + [rep_move(turned[k], x_pairs(k)) for k in range(1, x_count)]
    delta = call(
        functools.partial(delta_kernel, tp_count),
        like,
        [SM] + [VM] * (tp_count + 2),
        "delta",
        flops=tokens * width,
        nbytes=8 * tokens * width,
    )(info, *back_blocks, slope, delta1)
    rights = [delta] + [rep_move(delta, x_pairs(k)) for k in range(1, x_count)]
    chunk = jax.ShapeDtypeStruct((rows, width), BF)
    parts = call(
        functools.partial(part_kernel, x_count, z_count),
        (chunk,) * z_count,
        [SM] + [VM] * (2 * x_count),
        "part",
        scratch=[pltpu.VMEM((z_count, rows, width), BF)],
        flops=flops,
        nbytes=4 * feat * tokens,
    )(info, *lefts, *rights)
    sums = [parts[0]] + [rep_move(parts[k], z_pairs(k)) for k in range(1, z_count)]
    grad_rows = call(
        sum_kernel,
        jax.ShapeDtypeStruct((rows, width), F32),
        [VM] * z_count,
        "sum",
        flops=z_count * rows * width,
        nbytes=2 * z_count * rows * width,
    )(*sums)
    items = [x2] + [rep_move_last(x2, z_pairs(k)) for k in range(1, z_count)]
    pair = jax.ShapeDtypeStruct((WCAP, tokens, width), BF)
    tables = [pltpu.SMEM((replicas * WCAP,), jnp.int32), pltpu.SMEM((replicas,), jnp.int32)]
    slots = call(
        functools.partial(route_kernel, x_count, z_count),
        (pair,) * x_count,
        [SM, SM] + [VM] * z_count,
        "route",
        scratch=tables,
        nbytes=2 * z_count * tokens * width,
    )(info, wiring, *items)
    arrived = [slots[0]] + [rep_move_last(slots[k], x_pairs(k)) for k in range(1, x_count)]
    acts = call(
        functools.partial(place_kernel, x_count, z_count),
        pair,
        [SM, SM] + [VM] * (x_count + 1),
        "place",
        scratch=tables,
        nbytes=2 * z_count * tokens * width,
    )(info, wiring, x1, *arrived)
    return (
        acts.reshape(1, 1, 1, WCAP, tokens, width),
        grad_rows.reshape(1, rows, width),
    )


def solution(mesh):
    in_specs = (
        P(None, "rep", None, "tp"),
        P("section", None, "tp"),
        P(),
        P(),
        P(None, "rep", None, "tp"),
    )
    out_specs = (P("section", None, "rep", None, None, "tp"), P("section", "rep", "tp"))
    x_count = 4
    z_count = mesh.shape["rep"] // x_count
    return jax.shard_map(
        functools.partial(on_device, x_count, z_count),
        mesh=mesh,
        in_specs=in_specs,
        out_specs=out_specs,
        check_vma=False,
    )
```

```python
import functools
import math

import jax
import jax.numpy as jnp
from jax import lax
from jax.experimental import pallas as pl
from jax.experimental.pallas import tpu as pltpu
from jax.sharding import PartitionSpec as P

WCAP = 2
EPS = 1e-06
ROOT_HALF = 0.7071067811865476
NORMAL_PEAK = 0.3989422804014327
VMEM_LIMIT = 12 * 1024 * 1024
VM = pl.BlockSpec(memory_space=pltpu.VMEM)
SM = pl.BlockSpec(memory_space=pltpu.SMEM)
AWAY = ((0, 0), (1, 0), (2, 1), (0, 1), (1, 1), (0, 2), (1, 2), (2, 0))
BF = jnp.bfloat16
F32 = jnp.float32


def gelu_value(v):
    return 0.5 * v * (1.0 + lax.erf(v * ROOT_HALF))


def gelu_slope(v):
    return 0.5 * (1.0 + lax.erf(v * ROOT_HALF)) + v * jnp.exp(-0.5 * v * v) * NORMAL_PEAK


def call(body, out_shape, in_specs, name, scratch=(), flops=0, nbytes=0):
    many = isinstance(out_shape, (tuple, list))
    return pl.pallas_call(
        body,
        out_shape=out_shape,
        in_specs=in_specs,
        out_specs=tuple(VM for _ in out_shape) if many else VM,
        scratch_shapes=scratch,
        name=name,
        compiler_params=pltpu.CompilerParams(vmem_limit_bytes=VMEM_LIMIT),
        cost_estimate=pl.CostEstimate(flops=flops, bytes_accessed=nbytes, transcendentals=0),
    )


def rows_scale(blocks, feat):
    total = None
    for block in blocks:
        wide = block[...].astype(F32)
        part = jnp.sum(wide * wide, axis=-1, keepdims=True)
        total = part if total is None else total + part
    return lax.rsqrt(total / feat + EPS)


def weight_rows(w_ref, k, tp_pos, tp_count, width):
    start = pl.multiple_of(lax.rem(tp_pos + tp_count - k, tp_count) * width, width)
    return w_ref[pl.ds(start, width), :]


def rows_product(refs, w_ref, tp_pos, tp_count):
    width = refs[0].shape[-1]
    total = None
    for k, ref in enumerate(refs):
        part = jnp.dot(
            ref[...], weight_rows(w_ref, k, tp_pos, tp_count, width), preferred_element_type=F32
        )
        total = part if total is None else total + part
    return total


def first_kernel(tp_count, feat, info, _, *refs):
    blocks = refs[:tp_count]
    own_ref, other_ref, x1_ref, mixed_ref, scale_ref = refs[tp_count:]

    def run(w_ref):
        scale = rows_scale(blocks, feat)
        mixed = rows_product(blocks, w_ref, info[2], tp_count) * scale
        x1_ref[...] = (blocks[0][...].astype(F32) + gelu_value(mixed)).astype(BF)
        mixed_ref[...] = mixed
        scale_ref[...] = jnp.broadcast_to(scale, scale_ref.shape)

    @pl.when(info[0] == 0)
    def _():
        run(own_ref)

    @pl.when(info[0] == 1)
    def _():
        run(other_ref)


def second_kernel(tp_count, feat, loss_scale, info, lengths, *refs):
    early = refs[:tp_count]
    blocks = refs[tp_count : 2 * tp_count]
    own_ref, other_ref, goal_ref, x2_ref, delta_ref, pack_ref = refs[2 * tp_count : 2 * tp_count + 6]
    back_refs = refs[2 * tp_count + 6 :]
    tokens, width = blocks[0].shape
    tp_pos = info[2]

    def run(w_ref, base):
        scale = rows_scale(blocks, feat)
        mixed = rows_product(blocks, w_ref, tp_pos, tp_count) * scale
        x2 = (blocks[0][...].astype(F32) + gelu_value(mixed)).astype(BF)
        x2_ref[...] = x2
        token_ids = lax.broadcasted_iota(jnp.int32, (tokens, 1), 0) + base
        valid = jnp.where(token_ids < lengths[0, info[1]], loss_scale, 0.0)
        goal = goal_ref[base : base + tokens]
        grad = ((x2.astype(F32) - goal.astype(F32)) * valid).astype(BF)
        delta = (grad.astype(F32) * gelu_slope(mixed)).astype(BF)
        wide_delta = delta.astype(F32)
        stat = jnp.sum(mixed * wide_delta, axis=-1, keepdims=True) / feat
        delta_ref[...] = (wide_delta * scale).astype(BF)
        for k in range(tp_count):
            back = lax.dot_general(
                delta,
                weight_rows(w_ref, k, tp_pos, tp_count, width),
                (((1,), (1,)), ((), ())),
                preferred_element_type=F32,
            )
            row = scale * (back - blocks[k][...].astype(F32) * (scale * stat))
            if k == 0:
                row = row + grad.astype(F32)
            back_refs[k][...] = row.astype(BF)

    def pack(source):
        for k in range(tp_count):
            pack_ref[:, k * width : (k + 1) * width] = source[k][...]

    @pl.when(info[0] == 0)
    def _():
        run(other_ref, 0)
        pack(blocks)

    @pl.when(info[0] == 1)
    def _():
        run(own_ref, tokens)
        pack(early)


def turn_kernel(tp_count, x_count, info, *refs):
    first = refs[:tp_count]
    second = refs[tp_count : 2 * tp_count]
    other_ref, mixed_ref, scale_ref = refs[2 * tp_count : 2 * tp_count + 3]
    outs = refs[2 * tp_count + 3 : 2 * tp_count + 3 + x_count]
    slope_ref, turned = refs[2 * tp_count + 3 + x_count :]
    tp_pos = info[2]
    x_pos = lax.rem(info[1], x_count)
    rows = turned.shape[2]
    width = first[0].shape[1]

    def put(blocks):
        for k in range(tp_count):
            source = lax.rem(tp_pos + tp_count - k, tp_count)
            both = jnp.concatenate(
                [blocks[k][...], other_ref[:, k * width : (k + 1) * width]], axis=0
            )
            flipped = both.T
            per = width // rows
            for i in range(per):
                place = source * (per // x_count) + i // x_count
                turned[i % x_count, place] = flipped[i * rows : (i + 1) * rows]

    @pl.when(info[0] == 0)
    def _():
        put(first)

    @pl.when(info[0] == 1)
    def _():
        put(second)

    slope_ref[...] = gelu_slope(mixed_ref[...]) * scale_ref[:, :1]
    for k in range(x_count):
        outs[k][...] = turned[lax.rem(x_pos + k, x_count)].reshape(outs[k].shape)


def delta_kernel(tp_count, info, *refs):
    back, (slope_ref, last_ref, keep_ref, send_ref) = refs[:tp_count], refs[tp_count:]
    grad = back[0][...].astype(F32)
    for ref in back[1:]:
        grad = grad + ref[...].astype(F32)
    grad = grad.astype(BF).astype(F32)
    delta = (grad * slope_ref[...]).astype(BF)

    @pl.when(info[0] == 0)
    def _():
        keep_ref[...] = delta
        send_ref[...] = last_ref[...]

    @pl.when(info[0] == 1)
    def _():
        keep_ref[...] = last_ref[...]
        send_ref[...] = delta


def stack_kernel(*refs):
    for k, ref in enumerate(refs[:-1]):
        refs[-1][k] = ref[...]


def join_kernel(a_ref, b_ref, out_ref):
    half = a_ref.shape[0]
    out_ref[:half] = a_ref[...]
    out_ref[half:] = b_ref[...]


def part_kernel(x_count, z_count, info, *refs):
    turned, deltas = refs[:x_count], refs[x_count : 2 * x_count]
    own_ref, plus_ref, minus_ref, far_ref, wide_ref, parts = refs[2 * x_count :]
    left = jnp.concatenate([t[...] for t in turned], axis=1)
    right = jnp.concatenate([d[...] for d in deltas], axis=0)
    part = jnp.dot(left, right, preferred_element_type=F32).astype(BF)
    parts[...] = part.reshape(parts.shape)
    z_pos = info[1] // x_count

    def chunk(k):
        return parts[lax.rem(z_pos + z_count + k, z_count)]

    own_ref[...] = chunk(0)
    for i, k in enumerate((1, 4, -2)):
        plus_ref[i] = chunk(k)
    for i, k in enumerate((-1, 2)):
        minus_ref[i] = chunk(k)
    far_ref[...] = chunk(3)
    wide_ref[...] = chunk(-3)


def middle_kernel(plus_ref, minus_ref, far_ref, wide_ref, up_ref, down_ref):
    up = far_ref[...].astype(F32) + plus_ref[1].astype(F32) + minus_ref[1].astype(F32)
    up_ref[...] = up.astype(BF)
    down_ref[...] = (wide_ref[...].astype(F32) + plus_ref[2].astype(F32)).astype(BF)


def sum_kernel(own_ref, plus_ref, minus_ref, up_ref, down_ref, out_ref):
    total = own_ref[...].astype(F32) + plus_ref[0].astype(F32) + minus_ref[0].astype(F32)
    out_ref[...] = total + up_ref[...].astype(F32) + down_ref[...].astype(F32)


def table_kernel(x_count, z_count, info, wiring, _, out, table, counts):
    replicas = x_count * z_count
    fill_table(wiring, table, counts, replicas)
    x_pos = lax.rem(info[1], x_count)
    z_pos = info[1] // x_count
    for k in range(x_count):
        target = z_pos * x_count + lax.rem(x_pos + k, x_count)
        for c in range(WCAP):
            j = table[target * WCAP + c]
            here = (j >= 0) & (lax.rem(j, x_count) == x_pos)
            steps = lax.rem(z_pos + z_count - j // x_count, z_count)
            out[k * WCAP + c] = jnp.where(here, steps, -1)
    for c in range(WCAP):
        j = table[info[1] * WCAP + c]
        steps = lax.rem(x_pos + x_count - lax.rem(j, x_count), x_count)
        out[x_count * WCAP + c] = jnp.where(j >= 0, steps, -1)


def fill_table(wiring, table, counts, replicas):
    @pl.loop(0, replicas)
    def _(r):
        counts[r] = 0
        for c in range(WCAP):
            table[r * WCAP + c] = -1

    @pl.loop(0, replicas)
    def _(j):
        r = wiring[0, 0, j]
        table[r * WCAP + counts[r]] = j
        counts[r] = counts[r] + 1


def route_kernel(x_count, z_count, plan, *refs):
    near, outs = refs[:3], refs[3:]
    for k in range(x_count):
        for c in range(WCAP):
            steps = plan[k * WCAP + c]
            for m, (group, place) in enumerate(AWAY):

                @pl.when(steps == m)
                def _(k=k, c=c, group=group, place=place):
                    outs[k][c] = near[group][place]


def pick_kernel(x_count, info, plan, x1_ref, *refs):
    slots, (keep_ref, send_ref) = refs[:x_count], refs[x_count:]

    def place(out_ref):
        for c in range(WCAP):
            steps = plan[x_count * WCAP + c]

            @pl.when(steps < 0)
            def _(c=c):
                out_ref[c] = jnp.zeros_like(x1_ref)

            for k in range(x_count):

                @pl.when(steps == k)
                def _(c=c, k=k):
                    out_ref[c] = slots[k][c]

    def entry(out_ref):
        out_ref[0] = x1_ref[...]
        for c in range(1, WCAP):
            out_ref[c] = jnp.zeros_like(x1_ref)

    @pl.when(info[0] == 0)
    def _():
        entry(keep_ref)
        place(send_ref)

    @pl.when(info[0] == 1)
    def _():
        place(keep_ref)
        entry(send_ref)


def acts_kernel(info, keep_ref, come_ref, out_ref):
    half = keep_ref.shape[1]

    @pl.when(info[0] == 0)
    def _():
        out_ref[:, :half] = keep_ref[...]
        out_ref[:, half:] = come_ref[...]

    @pl.when(info[0] == 1)
    def _():
        out_ref[:, :half] = come_ref[...]
        out_ref[:, half:] = keep_ref[...]


def on_device(x_count, z_count, inputs, weights, wiring, lengths, targets):
    replicas = lax.axis_size("rep")
    tp_count = lax.axis_size("tp")
    section = lax.axis_index("section")
    rep = lax.axis_index("rep")
    tp = lax.axis_index("tp")
    info = jnp.stack([section, rep, tp]).astype(jnp.int32)
    _, _, tokens, width = inputs.shape
    half = tokens // 2
    weight = weights[0]
    feat = weight.shape[0]
    goal = targets.reshape(tokens, width)
    rows = feat // replicas
    loss_scale = 1.0 / math.sqrt(replicas * tokens)

    def swap(value):
        return lax.ppermute(value, "section", [(0, 1), (1, 0)])

    def tp_move(value, k):
        return lax.ppermute(value, "tp", [(y, (y + k) % tp_count) for y in range(tp_count)])

    def x_move(value, k):
        pairs = [
            (z * x_count + x, z * x_count + (x + k) % x_count)
            for z in range(z_count)
            for x in range(x_count)
        ]
        return lax.ppermute(value, "rep", pairs)

    def z_move(value, k):
        pairs = [
            (z * x_count + x, ((z + k) % z_count) * x_count + x)
            for z in range(z_count)
            for x in range(x_count)
        ]
        return lax.ppermute(value, "rep", pairs)

    def shape(*dims, dtype=BF):
        return jax.ShapeDtypeStruct(dims, dtype)

    flops = 2 * half * feat * width
    other_weight = swap(weight)
    plan = pl.pallas_call(
        functools.partial(table_kernel, x_count, z_count),
        out_shape=shape(x_count * WCAP + WCAP, dtype=jnp.int32),
        in_specs=[SM, SM, VM],
        out_specs=SM,
        scratch_shapes=[
            pltpu.SMEM((replicas * WCAP,), jnp.int32),
            pltpu.SMEM((replicas,), jnp.int32),
        ],
        name="table",
        compiler_params=pltpu.CompilerParams(vmem_limit_bytes=VMEM_LIMIT),
    )(info, wiring, weight)
    x0 = lax.dynamic_slice(inputs.reshape(tokens, width), (section * half, 0), (half, width))
    first_blocks = [x0] + [tp_move(x0, k) for k in range(1, tp_count)]
    x1, mixed, scale = call(
        functools.partial(first_kernel, tp_count, feat),
        (shape(half, width), shape(half, width, dtype=F32), shape(half, 128, dtype=F32)),
        [SM, SM] + [VM] * (tp_count + 2),
        "first",
        flops=flops,
        nbytes=2 * feat * width,
    )(info, plan, *first_blocks, weight, other_weight)
    second_blocks = [x1] + [tp_move(x1, k) for k in range(1, tp_count)]
    x2, delta1, packed, *back = call(
        functools.partial(second_kernel, tp_count, feat, loss_scale),
        (shape(half, width), shape(half, width), shape(half, feat))
        + (shape(half, width),) * tp_count,
        [SM, SM] + [VM] * (2 * tp_count + 3),
        "second",
        flops=2 * flops,
        nbytes=2 * feat * width,
    )(info, lengths, *first_blocks, *second_blocks, weight, other_weight, goal)
    back_blocks = [back[0]] + [tp_move(back[k], tp_count - k) for k in range(1, tp_count)]
    far = [x2, z_move(x2, 3), z_move(x2, z_count - 3)]
    trio = call(stack_kernel, shape(3, half, width), [VM] * 3, "trio")(*far)
    near = [trio, z_move(trio, 1), z_move(trio, z_count - 1)]
    other_pack = swap(packed)
    *turned, slope = call(
        functools.partial(turn_kernel, tp_count, x_count),
        (shape(feat // x_count, tokens),) * x_count + (shape(half, width, dtype=F32),),
        [SM] + [VM] * (2 * tp_count + 3),
        "turn",
        scratch=[pltpu.VMEM((x_count, z_count, rows, tokens), BF)],
        flops=flops // 4,
        nbytes=2 * feat * tokens,
    )(info, *first_blocks, *second_blocks, other_pack, mixed, scale)
    lefts = [turned[0]] + [x_move(turned[k], k) for k in range(1, x_count)]
    keep, send = call(
        functools.partial(delta_kernel, tp_count),
        (shape(half, width),) * 2,
        [SM] + [VM] * (tp_count + 2),
        "delta",
        flops=half * width,
        nbytes=8 * half * width,
    )(info, *back_blocks, slope, delta1)
    come = swap(send)
    delta = call(join_kernel, shape(tokens, width), [VM, VM], "join")(keep, come)
    rights = [delta] + [x_move(delta, k) for k in range(1, x_count)]
    chunk = shape(rows, width)
    own, plus, minus, far_part, wide_part = call(
        functools.partial(part_kernel, x_count, z_count),
        (chunk, shape(3, rows, width), shape(2, rows, width), chunk, chunk),
        [SM] + [VM] * (2 * x_count),
        "part",
        scratch=[pltpu.VMEM((z_count, rows, width), BF)],
        flops=2 * flops,
        nbytes=4 * feat * tokens,
    )(info, *lefts, *rights)
    plus, minus = z_move(plus, 1), z_move(minus, z_count - 1)
    up, down = call(middle_kernel, (chunk, chunk), [VM] * 4, "middle")(
        plus, minus, far_part, wide_part
    )
    grad_rows = call(sum_kernel, shape(rows, width, dtype=F32), [VM] * 5, "sum")(
        own, plus, minus, z_move(up, 3), z_move(down, z_count - 3)
    )
    pair = shape(WCAP, half, width)
    slots = call(
        functools.partial(route_kernel, x_count, z_count),
        (pair,) * x_count,
        [SM] + [VM] * 3,
        "route",
        nbytes=2 * z_count * half * width,
    )(plan, *near)
    arrived = [slots[0]] + [x_move(slots[k], k) for k in range(1, x_count)]
    held, sent = call(
        functools.partial(pick_kernel, x_count),
        (pair, pair),
        [SM, SM] + [VM] * (x_count + 1),
        "pick",
        nbytes=2 * z_count * half * width,
    )(info, plan, x1, *arrived)
    acts = call(acts_kernel, shape(WCAP, tokens, width), [SM, VM, VM], "acts")(
        info, held, swap(sent)
    )
    return (
        acts.reshape(1, 1, 1, WCAP, tokens, width),
        grad_rows.reshape(1, rows, width),
    )


def solution(mesh):
    in_specs = (
        P(None, "rep", None, "tp"),
        P("section", None, "tp"),
        P(),
        P(),
        P(None, "rep", None, "tp"),
    )
    out_specs = (P("section", None, "rep", None, None, "tp"), P("section", "rep", "tp"))
    x_count = 4
    z_count = mesh.shape["rep"] // x_count
    return jax.shard_map(
        functools.partial(on_device, x_count, z_count),
        mesh=mesh,
        in_specs=in_specs,
        out_specs=out_specs,
        check_vma=False,
    )
```

```python
import functools
import math

import jax
import jax.numpy as jnp
from jax import lax
from jax.experimental import pallas as pl
from jax.experimental.pallas import tpu as pltpu
from jax.sharding import PartitionSpec as P

WCAP = 2
EPS = 1e-06
ROOT_HALF = 0.7071067811865476
NORMAL_PEAK = 0.3989422804014327
VMEM_LIMIT = 12 * 1024 * 1024
VM = pl.BlockSpec(memory_space=pltpu.VMEM)
SM = pl.BlockSpec(memory_space=pltpu.SMEM)
AWAY = ((0, 0), (1, 0), (2, 1), (0, 1), (1, 1), (0, 2), (1, 2), (2, 0))
BF = jnp.bfloat16
F32 = jnp.float32


def gelu_value(v):
    return 0.5 * v * (1.0 + lax.erf(v * ROOT_HALF))


def gelu_slope(v):
    return 0.5 * (1.0 + lax.erf(v * ROOT_HALF)) + v * jnp.exp(-0.5 * v * v) * NORMAL_PEAK


def call(body, out_shape, in_specs, name, scratch=(), flops=0, nbytes=0):
    many = isinstance(out_shape, (tuple, list))
    return pl.pallas_call(
        body,
        out_shape=out_shape,
        in_specs=in_specs,
        out_specs=tuple(VM for _ in out_shape) if many else VM,
        scratch_shapes=scratch,
        name=name,
        compiler_params=pltpu.CompilerParams(vmem_limit_bytes=VMEM_LIMIT),
        cost_estimate=pl.CostEstimate(flops=flops, bytes_accessed=nbytes, transcendentals=0),
    )


def rows_scale(blocks, feat):
    total = None
    for block in blocks:
        wide = block[...].astype(F32)
        part = jnp.sum(wide * wide, axis=-1, keepdims=True)
        total = part if total is None else total + part
    return lax.rsqrt(total / feat + EPS)


def weight_rows(w_ref, k, tp_pos, tp_count, width):
    start = pl.multiple_of(lax.rem(tp_pos + tp_count - k, tp_count) * width, width)
    return w_ref[pl.ds(start, width), :]


def rows_product(refs, w_ref, tp_pos, tp_count):
    width = refs[0].shape[-1]
    total = None
    for k, ref in enumerate(refs):
        part = jnp.dot(
            ref[...], weight_rows(w_ref, k, tp_pos, tp_count, width), preferred_element_type=F32
        )
        total = part if total is None else total + part
    return total


def first_kernel(tp_count, feat, info, _, *refs):
    blocks = refs[:tp_count]
    own_ref, other_ref, x1_ref, mixed_ref, scale_ref = refs[tp_count:]

    def run(w_ref):
        scale = rows_scale(blocks, feat)
        mixed = rows_product(blocks, w_ref, info[2], tp_count) * scale
        x1_ref[...] = (blocks[0][...].astype(F32) + gelu_value(mixed)).astype(BF)
        mixed_ref[...] = mixed
        scale_ref[...] = jnp.broadcast_to(scale, scale_ref.shape)

    @pl.when(info[0] == 0)
    def _():
        run(own_ref)

    @pl.when(info[0] == 1)
    def _():
        run(other_ref)


def second_kernel(tp_count, feat, loss_scale, info, lengths, *refs):
    early = refs[:tp_count]
    blocks = refs[tp_count : 2 * tp_count]
    own_ref, other_ref, goal_ref, x2_ref, delta_ref, pack_ref = refs[2 * tp_count : 2 * tp_count + 6]
    back_refs = refs[2 * tp_count + 6 :]
    tokens, width = blocks[0].shape
    tp_pos = info[2]

    def run(w_ref, base):
        scale = rows_scale(blocks, feat)
        mixed = rows_product(blocks, w_ref, tp_pos, tp_count) * scale
        x2 = (blocks[0][...].astype(F32) + gelu_value(mixed)).astype(BF)
        x2_ref[...] = x2
        token_ids = lax.broadcasted_iota(jnp.int32, (tokens, 1), 0) + base
        valid = jnp.where(token_ids < lengths[0, info[1]], loss_scale, 0.0)
        goal = goal_ref[base : base + tokens]
        grad = ((x2.astype(F32) - goal.astype(F32)) * valid).astype(BF)
        delta = (grad.astype(F32) * gelu_slope(mixed)).astype(BF)
        wide_delta = delta.astype(F32)
        stat = jnp.sum(mixed * wide_delta, axis=-1, keepdims=True) / feat
        delta_ref[...] = (wide_delta * scale).astype(BF)
        for k in range(tp_count):
            back = lax.dot_general(
                delta,
                weight_rows(w_ref, k, tp_pos, tp_count, width),
                (((1,), (1,)), ((), ())),
                preferred_element_type=F32,
            )
            row = scale * (back - blocks[k][...].astype(F32) * (scale * stat))
            if k == 0:
                row = row + grad.astype(F32)
            back_refs[k][...] = row.astype(BF)

    def pack(source):
        for k in range(tp_count):
            pack_ref[:, k * width : (k + 1) * width] = source[k][...]

    @pl.when(info[0] == 0)
    def _():
        run(other_ref, 0)
        pack(blocks)

    @pl.when(info[0] == 1)
    def _():
        run(own_ref, tokens)
        pack(early)


def turn_kernel(tp_count, x_count, info, *refs):
    first = refs[:tp_count]
    second = refs[tp_count : 2 * tp_count]
    other_ref, mixed_ref, scale_ref = refs[2 * tp_count : 2 * tp_count + 3]
    outs = refs[2 * tp_count + 3 : 2 * tp_count + 3 + x_count]
    slope_ref, turned = refs[2 * tp_count + 3 + x_count :]
    tp_pos = info[2]
    x_pos = lax.rem(info[1], x_count)
    rows = turned.shape[2]
    width = first[0].shape[1]

    def put(blocks):
        for k in range(tp_count):
            source = lax.rem(tp_pos + tp_count - k, tp_count)
            both = jnp.concatenate(
                [blocks[k][...], other_ref[:, k * width : (k + 1) * width]], axis=0
            )
            flipped = both.T
            per = width // rows
            for i in range(per):
                place = source * (per // x_count) + i // x_count
                turned[i % x_count, place] = flipped[i * rows : (i + 1) * rows]

    @pl.when(info[0] == 0)
    def _():
        put(first)

    @pl.when(info[0] == 1)
    def _():
        put(second)

    slope_ref[...] = gelu_slope(mixed_ref[...]) * scale_ref[:, :1]
    for k in range(x_count):
        chunk = turned[lax.rem(x_pos + k, x_count)]
        outs[k][: chunk.shape[0] * rows] = chunk.reshape(-1, chunk.shape[2])


def delta_kernel(tp_count, info, *refs):
    back = refs[:tp_count]
    slope_ref, last_ref, keep_ref, send_ref = refs[tp_count:]
    grad = back[0][...].astype(F32)
    for ref in back[1:]:
        grad = grad + ref[...].astype(F32)
    grad = grad.astype(BF).astype(F32)
    delta = (grad * slope_ref[...]).astype(BF)

    @pl.when(info[0] == 0)
    def _():
        keep_ref[...] = delta
        send_ref[...] = last_ref[...]

    @pl.when(info[0] == 1)
    def _():
        keep_ref[...] = last_ref[...]
        send_ref[...] = delta


def trio_kernel(a_ref, b_ref, c_ref, _, out_ref):
    for k, ref in enumerate((a_ref, b_ref, c_ref)):
        out_ref[k] = ref[...]


def join_kernel(a_ref, b_ref, *refs):
    out_ref = refs[-1]
    half = a_ref.shape[0]
    out_ref[:half] = a_ref[...]
    out_ref[half:] = b_ref[...]


def part_kernel(x_count, z_count, info, *refs):
    turned, deltas = refs[:x_count], refs[x_count : 2 * x_count]
    own_ref, plus_ref, minus_ref, far_ref, wide_ref, parts = refs[2 * x_count :]
    left = jnp.concatenate([t[...] for t in turned], axis=1)
    right = jnp.concatenate([d[...] for d in deltas], axis=0)
    part = jnp.dot(left, right, preferred_element_type=F32).astype(BF)
    parts[...] = part.reshape(parts.shape)
    z_pos = info[1] // x_count

    def chunk(k):
        return parts[lax.rem(z_pos + z_count + k, z_count)]

    width = far_ref.shape[1]
    split = plus_ref.shape[1] - 2 * width
    own_ref[...] = chunk(0)
    far_ref[...] = chunk(3)
    wide_ref[...] = chunk(-3)
    plus_ref[:, :width] = chunk(1)
    plus_ref[:, width : 2 * width] = chunk(-2)
    plus_ref[:, 2 * width :] = chunk(4)[:, :split]
    minus_ref[:, :width] = chunk(-1)
    minus_ref[:, width : 2 * width] = chunk(2)
    minus_ref[:, 2 * width :] = chunk(4)[:, split:]


def middle_kernel(plus_ref, minus_ref, far_ref, wide_ref, _, up_ref, down_ref):
    width = far_ref.shape[1]
    split = plus_ref.shape[1] - 2 * width
    up = far_ref[...].astype(F32) + minus_ref[:, width : 2 * width].astype(F32)
    down = wide_ref[...].astype(F32) + plus_ref[:, width : 2 * width].astype(F32)
    up_ref[:, :split] = (up[:, :split] + plus_ref[:, 2 * width :].astype(F32)).astype(BF)
    up_ref[:, split:] = up[:, split:].astype(BF)
    down_ref[:, :split] = down[:, :split].astype(BF)
    down_ref[:, split:] = (down[:, split:] + minus_ref[:, 2 * width :].astype(F32)).astype(BF)


def sum_kernel(own_ref, plus_ref, minus_ref, up_ref, down_ref, _, out_ref):
    width = own_ref.shape[1]
    total = own_ref[...].astype(F32) + plus_ref[:, :width].astype(F32)
    total = total + minus_ref[:, :width].astype(F32)
    out_ref[...] = total + up_ref[...].astype(F32) + down_ref[...].astype(F32)


def plan_kernel(x_count, z_count, info, wiring, _, plan, counts):
    x_pos = lax.rem(info[1], x_count)
    z_pos = info[1] // x_count
    for i in range(x_count * WCAP + WCAP):
        plan[i] = -1
    for i in range(x_count):
        counts[i] = 0
    for j in range(x_count * z_count):
        r = wiring[0, 0, j]

        @pl.when(r // x_count == z_pos)
        def _(j=j, r=r):
            column = lax.rem(r, x_count)
            slot = jnp.minimum(counts[column], WCAP - 1)
            counts[column] = slot + 1

            @pl.when(x_pos == j % x_count)
            def _():
                shift = lax.rem(column + x_count - x_pos, x_count)
                plan[shift * WCAP + slot] = lax.rem(z_pos + z_count - j // x_count, z_count)

            @pl.when(column == x_pos)
            def _():
                plan[x_count * WCAP + slot] = lax.rem(x_pos + x_count - j % x_count, x_count)


def route_kernel(x_count, z_count, plan, *refs):
    near, outs = refs[:3], refs[-x_count:]
    for k in range(x_count):
        for c in range(WCAP):
            steps = plan[k * WCAP + c]
            for m, (group, place) in enumerate(AWAY):

                @pl.when(steps == m)
                def _(k=k, c=c, group=group, place=place):
                    outs[k][c] = near[group][place]


def pick_kernel(x_count, info, plan, x1_ref, *refs):
    slots, send_ref = refs[:x_count], refs[-1]

    @pl.when(info[0] == 0)
    def _():
        for c in range(WCAP):
            steps = plan[x_count * WCAP + c]
            for k in range(x_count):

                @pl.when(steps == k)
                def _(c=c, k=k):
                    send_ref[c] = slots[k][c]

            @pl.when(steps < 0)
            def _(c=c):
                send_ref[c] = jnp.zeros_like(x1_ref)

    @pl.when(info[0] == 1)
    def _():
        send_ref[0] = x1_ref[...]
        for c in range(1, WCAP):
            send_ref[c] = jnp.zeros_like(x1_ref)


def acts_kernel(x_count, info, plan, x1_ref, come_ref, *refs):
    slots, (out_ref, blank, sems) = refs[:x_count], refs[x_count:]
    half = x1_ref.shape[0]

    def put(source, c, own):
        base = own * half
        place = out_ref.at[c, pl.ds(base, half), :]
        return pltpu.make_async_copy(source, place, sems.at[c * 2 + own])

    blank[...] = jnp.zeros_like(blank)

    @pl.when(info[0] == 0)
    def _():
        put(x1_ref, 0, 0).start()
        for c in range(1, WCAP):
            put(blank, c, 0).start()
        for c in range(WCAP):
            put(come_ref.at[c], c, 1).start()

    @pl.when(info[0] == 1)
    def _():
        for c in range(WCAP):
            put(come_ref.at[c], c, 0).start()
            steps = plan[x_count * WCAP + c]
            for k in range(x_count):

                @pl.when(steps == k)
                def _(c=c, k=k):
                    put(slots[k].at[c], c, 1).start()

            @pl.when(steps < 0)
            def _(c=c):
                put(blank, c, 1).start()

    for c in range(WCAP):
        for own in range(2):
            put(blank, c, own).wait()


def on_device(x_count, z_count, inputs, weights, wiring, lengths, targets):
    replicas = lax.axis_size("rep")
    tp_count = lax.axis_size("tp")
    section = lax.axis_index("section")
    rep = lax.axis_index("rep")
    tp = lax.axis_index("tp")
    info = jnp.stack([section, rep, tp]).astype(jnp.int32)
    _, _, tokens, width = inputs.shape
    half = tokens // 2
    weight = weights[0]
    feat = weight.shape[0]
    goal = targets.reshape(tokens, width)
    rows = feat // replicas
    loss_scale = 1.0 / math.sqrt(replicas * tokens)

    def swap(value, label):
        with jax.named_scope(label):
            return lax.ppermute(value, "section", [(0, 1), (1, 0)])

    def tp_move(value, k, label):
        pairs = [(y, (y + k) % tp_count) for y in range(tp_count)]
        with jax.named_scope(label):
            return lax.ppermute(value, "tp", pairs)

    def x_move(value, k, label):
        pairs = [
            (z * x_count + x, z * x_count + (x + k) % x_count)
            for z in range(z_count)
            for x in range(x_count)
        ]
        with jax.named_scope(label):
            return lax.ppermute(value, "rep", pairs)

    def z_move(value, k, label):
        pairs = [
            (z * x_count + x, ((z + k) % z_count) * x_count + x)
            for z in range(z_count)
            for x in range(x_count)
        ]
        with jax.named_scope(label):
            return lax.ppermute(value, "rep", pairs)

    def shape(*dims, dtype=BF):
        return jax.ShapeDtypeStruct(dims, dtype)

    flops = 2 * half * feat * width
    other_weight = swap(weight, "swap_weight")
    plan = pl.pallas_call(
        functools.partial(plan_kernel, x_count, z_count),
        out_shape=shape(x_count * WCAP + WCAP, dtype=jnp.int32),
        in_specs=[SM, SM, VM],
        out_specs=SM,
        scratch_shapes=[pltpu.SMEM((x_count,), jnp.int32)],
        name="plan",
        compiler_params=pltpu.CompilerParams(vmem_limit_bytes=VMEM_LIMIT),
    )(info, wiring, weight)
    x0 = lax.dynamic_slice(inputs.reshape(tokens, width), (section * half, 0), (half, width))
    first_blocks = [x0] + [tp_move(x0, k, "gather_x0") for k in range(1, tp_count)]
    x1, mixed, scale = call(
        functools.partial(first_kernel, tp_count, feat),
        (shape(half, width), shape(half, width, dtype=F32), shape(half, 128, dtype=F32)),
        [SM, SM] + [VM] * (tp_count + 2),
        "first",
        flops=flops,
        nbytes=2 * feat * width,
    )(info, plan, *first_blocks, weight, other_weight)
    second_blocks = [x1] + [tp_move(x1, k, "gather_x1") for k in range(1, tp_count)]
    x2, delta1, packed, *back = call(
        functools.partial(second_kernel, tp_count, feat, loss_scale),
        (shape(half, width), shape(half, width), shape(half, feat))
        + (shape(half, width),) * tp_count,
        [SM, SM] + [VM] * (2 * tp_count + 3),
        "second",
        flops=2 * flops,
        nbytes=2 * feat * width,
    )(info, lengths, *first_blocks, *second_blocks, weight, other_weight, goal)
    back_blocks = [back[0]] + [tp_move(back[k], tp_count - k, "sum_back") for k in range(1, tp_count)]
    other_pack = swap(packed, "swap_rows")
    *turned, slope = call(
        functools.partial(turn_kernel, tp_count, x_count),
        (shape(feat // x_count, tokens),) * x_count + (shape(half, width, dtype=F32),),
        [SM] + [VM] * (2 * tp_count + 3),
        "turn",
        scratch=[pltpu.VMEM((x_count, z_count, rows, tokens), BF)],
        flops=flops // 4,
        nbytes=2 * feat * tokens,
    )(info, *first_blocks, *second_blocks, other_pack, mixed, scale)
    far = [x2, z_move(x2, 3, "route_far"), z_move(x2, z_count - 3, "route_far")]
    lefts = [turned[0]] + [x_move(turned[k], k, "spread_rows") for k in range(1, x_count)]
    keep, send = call(
        functools.partial(delta_kernel, tp_count),
        (shape(half, width), shape(half, width)),
        [SM] + [VM] * (tp_count + 2),
        "delta",
        flops=half * width,
        nbytes=8 * half * width,
    )(info, *back_blocks, slope, delta1)
    come = swap(send, "swap_delta")
    delta = call(join_kernel, shape(tokens, width), [VM] * (4 + x_count), "join")(
        keep, come, *far, *lefts[1:]
    )
    rights = [delta] + [x_move(delta, k, "gather_delta") for k in range(1, x_count)]
    trio = call(trio_kernel, shape(3, half, width), [VM] * 4, "trio")(*far, rights[1])
    near = [
        trio,
        z_move(trio, 1, "route_near"),
        z_move(trio, z_count - 1, "route_near"),
    ]
    pair = shape(WCAP, half, width)
    slots = call(
        functools.partial(route_kernel, x_count, z_count),
        (pair,) * x_count,
        [SM] + [VM] * 3,
        "route",
        nbytes=2 * z_count * half * width,
    )(plan, *near)
    chunk = shape(rows, width)
    split = -(-width // 256) * 128
    own, plus, minus, far_part, wide_part = call(
        functools.partial(part_kernel, x_count, z_count),
        (chunk, shape(rows, 2 * width + split), shape(rows, 3 * width - split), chunk, chunk),
        [SM] + [VM] * (2 * x_count),
        "part",
        scratch=[pltpu.VMEM((z_count, rows, width), BF)],
        flops=2 * flops,
        nbytes=4 * feat * tokens,
    )(info, *lefts, *rights)
    plus, minus = z_move(plus, 1, "part_near"), z_move(minus, z_count - 1, "part_near")
    up, down = call(middle_kernel, (chunk, chunk), [VM] * 5, "middle")(
        plus, minus, far_part, wide_part, slots[0]
    )
    up, down = z_move(up, 3, "part_far"), z_move(down, z_count - 3, "part_far")
    arrived = [slots[0]] + [x_move(slots[k], k, "route_x") for k in range(1, x_count)]
    sent = call(
        functools.partial(pick_kernel, x_count),
        pair,
        [SM, SM] + [VM] * (x_count + 3),
        "pick",
        nbytes=2 * z_count * half * width,
    )(info, plan, x1, *arrived, up, down)
    grad_rows = call(sum_kernel, shape(rows, width, dtype=F32), [VM] * 6, "sum")(
        own, plus, minus, up, down, sent
    )
    acts = pl.pallas_call(
        functools.partial(acts_kernel, x_count),
        out_shape=shape(WCAP, tokens, width),
        in_specs=[SM, SM] + [VM] * (x_count + 2),
        out_specs=pl.BlockSpec(memory_space=pl.ANY),
        scratch_shapes=[
            pltpu.VMEM((half, width), BF),
            pltpu.SemaphoreType.DMA((2 * WCAP,)),
        ],
        name="acts",
        compiler_params=pltpu.CompilerParams(vmem_limit_bytes=VMEM_LIMIT),
    )(info, plan, x1, swap(sent, "swap_acts"), *arrived)
    return (
        acts.reshape(1, 1, 1, WCAP, tokens, width),
        grad_rows.reshape(1, rows, width),
    )


def solution(mesh):
    in_specs = (
        P(None, "rep", None, "tp"),
        P("section", None, "tp"),
        P(),
        P(),
        P(None, "rep", None, "tp"),
    )
    out_specs = (P("section", None, "rep", None, None, "tp"), P("section", "rep", "tp"))
    x_count = 4
    z_count = mesh.shape["rep"] // x_count
    return jax.shard_map(
        functools.partial(on_device, x_count, z_count),
        mesh=mesh,
        in_specs=in_specs,
        out_specs=out_specs,
        check_vma=False,
    )
```

```python
import functools
import math

import jax
import jax.numpy as jnp
from jax import lax
from jax.experimental import pallas as pl
from jax.experimental.pallas import tpu as pltpu
from jax.sharding import PartitionSpec as P

WCAP = 2
EPS = 1e-06
ROOT_HALF = 0.7071067811865476
NORMAL_PEAK = 0.3989422804014327
VMEM_LIMIT = 12 * 1024 * 1024
VM = pl.BlockSpec(memory_space=pltpu.VMEM)
SM = pl.BlockSpec(memory_space=pltpu.SMEM)
AWAY = ((0, 0), (1, 0), (2, 1), (0, 1), (1, 1), (0, 2), (1, 2), (2, 0))
BF = jnp.bfloat16
FILL = 20 * 10**9
F32 = jnp.float32


def gelu_value(v):
    return 0.5 * v * (1.0 + lax.erf(v * ROOT_HALF))


def gelu_slope(v):
    return 0.5 * (1.0 + lax.erf(v * ROOT_HALF)) + v * jnp.exp(-0.5 * v * v) * NORMAL_PEAK


def call(body, out_shape, in_specs, name, scratch=(), flops=0, nbytes=0):
    many = isinstance(out_shape, (tuple, list))
    return pl.pallas_call(
        body,
        out_shape=out_shape,
        in_specs=in_specs,
        out_specs=tuple(VM for _ in out_shape) if many else VM,
        scratch_shapes=scratch,
        name=name,
        compiler_params=pltpu.CompilerParams(vmem_limit_bytes=VMEM_LIMIT),
        cost_estimate=pl.CostEstimate(flops=flops, bytes_accessed=nbytes, transcendentals=0),
    )


def rows_scale(blocks, feat):
    total = None
    for block in blocks:
        wide = block[...].astype(F32)
        part = jnp.sum(wide * wide, axis=-1, keepdims=True)
        total = part if total is None else total + part
    return lax.rsqrt(total / feat + EPS)


def weight_rows(w_ref, k, tp_pos, tp_count, width):
    start = pl.multiple_of(lax.rem(tp_pos + tp_count - k, tp_count) * width, width)
    return w_ref[pl.ds(start, width), :]


def rows_product(refs, w_ref, tp_pos, tp_count):
    width = refs[0].shape[-1]
    total = None
    for k, ref in enumerate(refs):
        part = jnp.dot(
            ref[...], weight_rows(w_ref, k, tp_pos, tp_count, width), preferred_element_type=F32
        )
        total = part if total is None else total + part
    return total


def first_kernel(tp_count, feat, info, _, *refs):
    blocks = refs[:tp_count]
    own_ref, other_ref, x1_ref, mixed_ref, scale_ref = refs[tp_count:]

    def run(w_ref):
        scale = rows_scale(blocks, feat)
        mixed = rows_product(blocks, w_ref, info[2], tp_count) * scale
        x1_ref[...] = (blocks[0][...].astype(F32) + gelu_value(mixed)).astype(BF)
        mixed_ref[...] = mixed
        scale_ref[...] = jnp.broadcast_to(scale, scale_ref.shape)

    @pl.when(info[0] == 0)
    def _():
        run(own_ref)

    @pl.when(info[0] == 1)
    def _():
        run(other_ref)


def second_kernel(tp_count, feat, loss_scale, info, lengths, *refs):
    early = refs[:tp_count]
    blocks = refs[tp_count : 2 * tp_count]
    own_ref, other_ref, goal_ref, x2_ref, delta_ref, pack_ref = refs[2 * tp_count : 2 * tp_count + 6]
    back_refs = refs[2 * tp_count + 6 :]
    tokens, width = blocks[0].shape
    tp_pos = info[2]

    def run(w_ref, base):
        scale = rows_scale(blocks, feat)
        mixed = rows_product(blocks, w_ref, tp_pos, tp_count) * scale
        x2 = (blocks[0][...].astype(F32) + gelu_value(mixed)).astype(BF)
        x2_ref[...] = x2
        token_ids = lax.broadcasted_iota(jnp.int32, (tokens, 1), 0) + base
        valid = jnp.where(token_ids < lengths[0, info[1]], loss_scale, 0.0)
        goal = goal_ref[base : base + tokens]
        grad = ((x2.astype(F32) - goal.astype(F32)) * valid).astype(BF)
        delta = (grad.astype(F32) * gelu_slope(mixed)).astype(BF)
        wide_delta = delta.astype(F32)
        stat = jnp.sum(mixed * wide_delta, axis=-1, keepdims=True) / feat
        delta_ref[...] = (wide_delta * scale).astype(BF)
        for k in range(tp_count):
            back = lax.dot_general(
                delta,
                weight_rows(w_ref, k, tp_pos, tp_count, width),
                (((1,), (1,)), ((), ())),
                preferred_element_type=F32,
            )
            row = scale * (back - blocks[k][...].astype(F32) * (scale * stat))
            if k == 0:
                row = row + grad.astype(F32)
            back_refs[k][...] = row.astype(BF)

    def pack(source):
        for k in range(tp_count):
            pack_ref[:, k * width : (k + 1) * width] = source[k][...]

    @pl.when(info[0] == 0)
    def _():
        run(other_ref, 0)
        pack(blocks)

    @pl.when(info[0] == 1)
    def _():
        run(own_ref, tokens)
        pack(early)


def turn_kernel(tp_count, x_count, info, *refs):
    first = refs[:tp_count]
    second = refs[tp_count : 2 * tp_count]
    other_ref, mixed_ref, scale_ref = refs[2 * tp_count : 2 * tp_count + 3]
    outs = refs[2 * tp_count + 3 : 2 * tp_count + 3 + x_count]
    slope_ref, turned = refs[2 * tp_count + 3 + x_count :]
    tp_pos = info[2]
    x_pos = lax.rem(info[1], x_count)
    rows = turned.shape[2]
    width = first[0].shape[1]

    def put(blocks):
        for k in range(tp_count):
            source = lax.rem(tp_pos + tp_count - k, tp_count)
            both = jnp.concatenate(
                [blocks[k][...], other_ref[:, k * width : (k + 1) * width]], axis=0
            )
            flipped = both.T
            per = width // rows
            for i in range(per):
                place = source * (per // x_count) + i // x_count
                turned[i % x_count, place] = flipped[i * rows : (i + 1) * rows]

    @pl.when(info[0] == 0)
    def _():
        put(first)

    @pl.when(info[0] == 1)
    def _():
        put(second)

    slope_ref[...] = gelu_slope(mixed_ref[...]) * scale_ref[:, :1]
    for k in range(x_count):
        chunk = turned[lax.rem(x_pos + k, x_count)]
        outs[k][: chunk.shape[0] * rows] = chunk.reshape(-1, chunk.shape[2])


def delta_kernel(tp_count, info, *refs):
    back = refs[:tp_count]
    slope_ref, last_ref, keep_ref, send_ref = refs[tp_count:]
    grad = back[0][...].astype(F32)
    for ref in back[1:]:
        grad = grad + ref[...].astype(F32)
    grad = grad.astype(BF).astype(F32)
    delta = (grad * slope_ref[...]).astype(BF)

    @pl.when(info[0] == 0)
    def _():
        keep_ref[...] = delta
        send_ref[...] = last_ref[...]

    @pl.when(info[0] == 1)
    def _():
        keep_ref[...] = last_ref[...]
        send_ref[...] = delta


def join_kernel(a_ref, b_ref, *refs):
    out_ref, trio_ref = refs[-2:]
    for k in range(3):
        trio_ref[k] = refs[k][...]
    half = a_ref.shape[0]
    out_ref[:half] = a_ref[...]
    out_ref[half:] = b_ref[...]


def part_kernel(x_count, z_count, info, *refs):
    turned, deltas = refs[:x_count], refs[x_count : 2 * x_count]
    own_ref, plus_ref, minus_ref, far_ref, wide_ref, parts = refs[2 * x_count + 1 :]
    left = jnp.concatenate([t[...] for t in turned], axis=1)
    right = jnp.concatenate([d[...] for d in deltas], axis=0)
    part = jnp.dot(left, right, preferred_element_type=F32).astype(BF)
    parts[...] = part.reshape(parts.shape)
    z_pos = info[1] // x_count

    def chunk(k):
        return parts[lax.rem(z_pos + z_count + k, z_count)]

    width = far_ref.shape[1]
    split = plus_ref.shape[1] - 2 * width
    own_ref[...] = chunk(0)
    far_ref[...] = chunk(3)
    wide_ref[...] = chunk(-3)
    plus_ref[:, :width] = chunk(1)
    plus_ref[:, width : 2 * width] = chunk(-2)
    plus_ref[:, 2 * width :] = chunk(4)[:, :split]
    minus_ref[:, :width] = chunk(-1)
    minus_ref[:, width : 2 * width] = chunk(2)
    minus_ref[:, 2 * width :] = chunk(4)[:, split:]


def middle_kernel(plus_ref, minus_ref, far_ref, wide_ref, up_ref, down_ref):
    width = far_ref.shape[1]
    split = plus_ref.shape[1] - 2 * width
    up = far_ref[...].astype(F32) + minus_ref[:, width : 2 * width].astype(F32)
    down = wide_ref[...].astype(F32) + plus_ref[:, width : 2 * width].astype(F32)
    up_ref[:, :split] = (up[:, :split] + plus_ref[:, 2 * width :].astype(F32)).astype(BF)
    up_ref[:, split:] = up[:, split:].astype(BF)
    down_ref[:, :split] = down[:, :split].astype(BF)
    down_ref[:, split:] = (down[:, split:] + minus_ref[:, 2 * width :].astype(F32)).astype(BF)


def sum_kernel(own_ref, plus_ref, minus_ref, up_ref, down_ref, out_ref):
    width = own_ref.shape[1]
    total = own_ref[...].astype(F32) + plus_ref[:, :width].astype(F32)
    total = total + minus_ref[:, :width].astype(F32)
    out_ref[...] = total + up_ref[...].astype(F32) + down_ref[...].astype(F32)


def plan_kernel(x_count, z_count, info, wiring, _, plan, counts):
    x_pos = lax.rem(info[1], x_count)
    z_pos = info[1] // x_count
    for i in range(x_count * WCAP + WCAP):
        plan[i] = -1
    for i in range(x_count):
        counts[i] = 0
    for j in range(x_count * z_count):
        r = wiring[0, 0, j]

        @pl.when(r // x_count == z_pos)
        def _(j=j, r=r):
            column = lax.rem(r, x_count)
            slot = jnp.minimum(counts[column], WCAP - 1)
            counts[column] = slot + 1

            @pl.when(x_pos == j % x_count)
            def _():
                shift = lax.rem(column + x_count - x_pos, x_count)
                plan[shift * WCAP + slot] = lax.rem(z_pos + z_count - j // x_count, z_count)

            @pl.when(column == x_pos)
            def _():
                plan[x_count * WCAP + slot] = lax.rem(x_pos + x_count - j % x_count, x_count)


def route_kernel(x_count, z_count, plan, *refs):
    near, outs = refs[:3], refs[-x_count:]
    for k in range(x_count):
        for c in range(WCAP):
            steps = plan[k * WCAP + c]
            for m, (group, place) in enumerate(AWAY):

                @pl.when(steps == m)
                def _(k=k, c=c, group=group, place=place):
                    outs[k][c] = near[group][place]


def pick_kernel(x_count, info, plan, x1_ref, *refs):
    slots, send_ref = refs[:x_count], refs[-1]

    @pl.when(info[0] == 0)
    def _():
        for c in range(WCAP):
            steps = plan[x_count * WCAP + c]
            for k in range(x_count):

                @pl.when(steps == k)
                def _(c=c, k=k):
                    send_ref[c] = slots[k][c]

            @pl.when(steps < 0)
            def _(c=c):
                send_ref[c] = jnp.zeros_like(x1_ref)

    @pl.when(info[0] == 1)
    def _():
        send_ref[0] = x1_ref[...]
        for c in range(1, WCAP):
            send_ref[c] = jnp.zeros_like(x1_ref)


def acts_kernel(x_count, info, plan, x1_ref, come_ref, *refs):
    slots, (out_ref, blank, sems) = refs[:x_count], refs[x_count:]
    half = x1_ref.shape[0]

    def put(source, c, own):
        base = own * half
        place = out_ref.at[c, pl.ds(base, half), :]
        return pltpu.make_async_copy(source, place, sems.at[c * 2 + own])

    blank[...] = jnp.zeros_like(blank)

    @pl.when(info[0] == 0)
    def _():
        put(x1_ref, 0, 0).start()
        for c in range(1, WCAP):
            put(blank, c, 0).start()
        for c in range(WCAP):
            put(come_ref.at[c], c, 1).start()

    @pl.when(info[0] == 1)
    def _():
        for c in range(WCAP):
            put(come_ref.at[c], c, 0).start()
            steps = plan[x_count * WCAP + c]
            for k in range(x_count):

                @pl.when(steps == k)
                def _(c=c, k=k):
                    put(slots[k].at[c], c, 1).start()

            @pl.when(steps < 0)
            def _(c=c):
                put(blank, c, 1).start()

    for c in range(WCAP):
        for own in range(2):
            put(blank, c, own).wait()


def on_device(x_count, z_count, inputs, weights, wiring, lengths, targets):
    replicas = lax.axis_size("rep")
    tp_count = lax.axis_size("tp")
    section = lax.axis_index("section")
    rep = lax.axis_index("rep")
    tp = lax.axis_index("tp")
    info = jnp.stack([section, rep, tp]).astype(jnp.int32)
    _, _, tokens, width = inputs.shape
    half = tokens // 2
    weight = weights[0]
    feat = weight.shape[0]
    goal = targets.reshape(tokens, width)
    rows = feat // replicas
    loss_scale = 1.0 / math.sqrt(replicas * tokens)

    def swap(value, label):
        with jax.named_scope(label):
            return lax.ppermute(value, "section", [(0, 1), (1, 0)])

    def tp_move(value, k, label):
        pairs = [(y, (y + k) % tp_count) for y in range(tp_count)]
        with jax.named_scope(label):
            return lax.ppermute(value, "tp", pairs)

    def x_move(value, k, label):
        pairs = [
            (z * x_count + x, z * x_count + (x + k) % x_count)
            for z in range(z_count)
            for x in range(x_count)
        ]
        with jax.named_scope(label):
            return lax.ppermute(value, "rep", pairs)

    def z_move(value, k, label):
        pairs = [
            (z * x_count + x, ((z + k) % z_count) * x_count + x)
            for z in range(z_count)
            for x in range(x_count)
        ]
        with jax.named_scope(label):
            return lax.ppermute(value, "rep", pairs)

    def shape(*dims, dtype=BF):
        return jax.ShapeDtypeStruct(dims, dtype)

    flops = 2 * half * feat * width
    other_weight = swap(weight, "swap_weight")
    plan = pl.pallas_call(
        functools.partial(plan_kernel, x_count, z_count),
        out_shape=shape(x_count * WCAP + WCAP, dtype=jnp.int32),
        in_specs=[SM, SM, VM],
        out_specs=SM,
        scratch_shapes=[pltpu.SMEM((x_count,), jnp.int32)],
        name="plan",
        compiler_params=pltpu.CompilerParams(vmem_limit_bytes=VMEM_LIMIT),
    )(info, wiring, weight)
    x0 = lax.dynamic_slice(inputs.reshape(tokens, width), (section * half, 0), (half, width))
    first_blocks = [x0] + [tp_move(x0, k, "gather_x0") for k in range(1, tp_count)]
    x1, mixed, scale = call(
        functools.partial(first_kernel, tp_count, feat),
        (shape(half, width), shape(half, width, dtype=F32), shape(half, 128, dtype=F32)),
        [SM, SM] + [VM] * (tp_count + 2),
        "first",
        flops=flops,
        nbytes=2 * feat * width,
    )(info, plan, *first_blocks, weight, other_weight)
    second_blocks = [x1] + [tp_move(x1, k, "gather_x1") for k in range(1, tp_count)]
    x2, delta1, packed, *back = call(
        functools.partial(second_kernel, tp_count, feat, loss_scale),
        (shape(half, width), shape(half, width), shape(half, feat))
        + (shape(half, width),) * tp_count,
        [SM, SM] + [VM] * (2 * tp_count + 3),
        "second",
        flops=2 * flops,
        nbytes=2 * feat * width,
    )(info, lengths, *first_blocks, *second_blocks, weight, other_weight, goal)
    back_blocks = [back[0]] + [tp_move(back[k], tp_count - k, "sum_back") for k in range(1, tp_count)]
    other_pack = swap(packed, "swap_rows")
    *turned, slope = call(
        functools.partial(turn_kernel, tp_count, x_count),
        (shape(feat // x_count, tokens),) * x_count + (shape(half, width, dtype=F32),),
        [SM] + [VM] * (2 * tp_count + 3),
        "turn",
        scratch=[pltpu.VMEM((x_count, z_count, rows, tokens), BF)],
        flops=flops // 4,
        nbytes=2 * feat * tokens,
    )(info, *first_blocks, *second_blocks, other_pack, mixed, scale)
    far = [x2, z_move(x2, 3, "route_far"), z_move(x2, z_count - 3, "route_far")]
    lefts = [turned[0]] + [x_move(turned[k], k, "spread_rows") for k in range(1, x_count)]
    keep, send = call(
        functools.partial(delta_kernel, tp_count),
        (shape(half, width), shape(half, width)),
        [SM] + [VM] * (tp_count + 2),
        "delta",
        flops=half * width,
        nbytes=8 * half * width,
    )(info, *back_blocks, slope, delta1)
    come = swap(send, "swap_delta")
    delta, trio = call(
        join_kernel,
        (shape(tokens, width), shape(3, half, width)),
        [VM] * (4 + x_count),
        "join",
    )(keep, come, *far, *lefts[1:])
    rights = [delta] + [x_move(delta, k, "gather_delta") for k in range(1, x_count)]
    near = [
        trio,
        z_move(trio, 1, "route_near"),
        z_move(trio, z_count - 1, "route_near"),
    ]
    pair = shape(WCAP, half, width)
    slots = call(
        functools.partial(route_kernel, x_count, z_count),
        (pair,) * x_count,
        [SM] + [VM] * 3,
        "route",
        nbytes=2 * z_count * half * width,
    )(plan, *near)
    chunk = shape(rows, width)
    split = -(-width // 256) * 128
    own, plus, minus, far_part, wide_part = call(
        functools.partial(part_kernel, x_count, z_count),
        (chunk, shape(rows, 2 * width + split), shape(rows, 3 * width - split), chunk, chunk),
        [SM] + [VM] * (2 * x_count + 1),
        "part",
        scratch=[pltpu.VMEM((z_count, rows, width), BF)],
        flops=2 * flops,
        nbytes=4 * feat * tokens,
    )(info, *lefts, *rights, slots[0])
    plus, minus = z_move(plus, 1, "part_near"), z_move(minus, z_count - 1, "part_near")
    up, down = call(middle_kernel, (chunk, chunk), [VM] * 4, "middle")(
        plus, minus, far_part, wide_part
    )
    up, down = z_move(up, 3, "part_far"), z_move(down, z_count - 3, "part_far")
    arrived = [slots[0]] + [x_move(slots[k], k, "route_x") for k in range(1, x_count)]
    sent = call(
        functools.partial(pick_kernel, x_count),
        pair,
        [SM, SM] + [VM] * (x_count + 1),
        "pick",
        flops=FILL,
        nbytes=2 * z_count * half * width,
    )(info, plan, x1, *arrived)
    grad_rows = call(sum_kernel, shape(rows, width, dtype=F32), [VM] * 5, "sum")(
        own, plus, minus, up, down
    )
    acts = pl.pallas_call(
        functools.partial(acts_kernel, x_count),
        out_shape=shape(WCAP, tokens, width),
        in_specs=[SM, SM] + [VM] * (x_count + 2),
        out_specs=pl.BlockSpec(memory_space=pl.ANY),
        scratch_shapes=[
            pltpu.VMEM((half, width), BF),
            pltpu.SemaphoreType.DMA((2 * WCAP,)),
        ],
        name="acts",
        compiler_params=pltpu.CompilerParams(vmem_limit_bytes=VMEM_LIMIT),
    )(info, plan, x1, swap(sent, "swap_acts"), *arrived)
    return (
        acts.reshape(1, 1, 1, WCAP, tokens, width),
        grad_rows.reshape(1, rows, width),
    )


def solution(mesh):
    in_specs = (
        P(None, "rep", None, "tp"),
        P("section", None, "tp"),
        P(),
        P(),
        P(None, "rep", None, "tp"),
    )
    out_specs = (P("section", None, "rep", None, None, "tp"), P("section", "rep", "tp"))
    x_count = 4
    z_count = mesh.shape["rep"] // x_count
    return jax.shard_map(
        functools.partial(on_device, x_count, z_count),
        mesh=mesh,
        in_specs=in_specs,
        out_specs=out_specs,
        check_vma=False,
    )
```

```python
import functools
import math

import jax
import jax.numpy as jnp
from jax import lax
from jax.experimental import pallas as pl
from jax.experimental.pallas import tpu as pltpu
from jax.sharding import PartitionSpec as P

WCAP = 2
EPS = 1e-06
ROOT_HALF = 0.7071067811865476
NORMAL_PEAK = 0.3989422804014327
VMEM_LIMIT = 12 * 1024 * 1024
VM = pl.BlockSpec(memory_space=pltpu.VMEM)
SM = pl.BlockSpec(memory_space=pltpu.SMEM)
AWAY = ((0, 0), (1, 0), (2, 1), (0, 1), (1, 1), (0, 2), (1, 2), (2, 0))
BF = jnp.bfloat16
FILL = 20 * 10**9
F32 = jnp.float32


def gelu_value(v):
    return 0.5 * v * (1.0 + lax.erf(v * ROOT_HALF))


def gelu_slope(v):
    return 0.5 * (1.0 + lax.erf(v * ROOT_HALF)) + v * jnp.exp(-0.5 * v * v) * NORMAL_PEAK


def call(body, out_shape, in_specs, name, scratch=(), flops=0, nbytes=0):
    many = isinstance(out_shape, (tuple, list))
    return pl.pallas_call(
        body,
        out_shape=out_shape,
        in_specs=in_specs,
        out_specs=tuple(VM for _ in out_shape) if many else VM,
        scratch_shapes=scratch,
        name=name,
        compiler_params=pltpu.CompilerParams(vmem_limit_bytes=VMEM_LIMIT),
        cost_estimate=pl.CostEstimate(flops=flops, bytes_accessed=nbytes, transcendentals=0),
    )


def rows_scale(blocks, feat):
    total = None
    for block in blocks:
        wide = block[...].astype(F32)
        part = jnp.sum(wide * wide, axis=-1, keepdims=True)
        total = part if total is None else total + part
    return lax.rsqrt(total / feat + EPS)


def weight_rows(w_ref, k, tp_pos, tp_count, width):
    start = pl.multiple_of(lax.rem(tp_pos + tp_count - k, tp_count) * width, width)
    return w_ref[pl.ds(start, width), :]


def rows_product(refs, w_ref, tp_pos, tp_count):
    width = refs[0].shape[-1]
    total = None
    for k, ref in enumerate(refs):
        part = jnp.dot(
            ref[...], weight_rows(w_ref, k, tp_pos, tp_count, width), preferred_element_type=F32
        )
        total = part if total is None else total + part
    return total


def first_kernel(tp_count, feat, info, _, *refs):
    blocks = refs[:tp_count]
    own_ref, other_ref, x1_ref, mixed_ref, scale_ref = refs[tp_count:]

    def run(w_ref):
        scale = rows_scale(blocks, feat)
        mixed = rows_product(blocks, w_ref, info[2], tp_count) * scale
        x1_ref[...] = (blocks[0][...].astype(F32) + gelu_value(mixed)).astype(BF)
        mixed_ref[...] = mixed
        scale_ref[...] = jnp.broadcast_to(scale, scale_ref.shape)

    @pl.when(info[0] == 0)
    def _():
        run(own_ref)

    @pl.when(info[0] == 1)
    def _():
        run(other_ref)


def second_kernel(tp_count, feat, loss_scale, info, lengths, _, *refs):
    early = refs[:tp_count]
    blocks = refs[tp_count : 2 * tp_count]
    own_ref, other_ref, goal_ref, x2_ref, delta_ref, pack_ref = refs[2 * tp_count : 2 * tp_count + 6]
    back_refs = refs[2 * tp_count + 6 :]
    tokens, width = blocks[0].shape
    tp_pos = info[2]

    def run(w_ref, base):
        scale = rows_scale(blocks, feat)
        mixed = rows_product(blocks, w_ref, tp_pos, tp_count) * scale
        x2 = (blocks[0][...].astype(F32) + gelu_value(mixed)).astype(BF)
        x2_ref[...] = x2
        token_ids = lax.broadcasted_iota(jnp.int32, (tokens, 1), 0) + base
        valid = jnp.where(token_ids < lengths[0, info[1]], loss_scale, 0.0)
        goal = goal_ref[base : base + tokens]
        grad = ((x2.astype(F32) - goal.astype(F32)) * valid).astype(BF)
        delta = (grad.astype(F32) * gelu_slope(mixed)).astype(BF)
        wide_delta = delta.astype(F32)
        stat = jnp.sum(mixed * wide_delta, axis=-1, keepdims=True) / feat
        delta_ref[...] = (wide_delta * scale).astype(BF)
        for k in range(tp_count):
            back = lax.dot_general(
                delta,
                weight_rows(w_ref, k, tp_pos, tp_count, width),
                (((1,), (1,)), ((), ())),
                preferred_element_type=F32,
            )
            row = scale * (back - blocks[k][...].astype(F32) * (scale * stat))
            if k == 0:
                row = row + grad.astype(F32)
            back_refs[k][...] = row.astype(BF)

    def pack(source):
        for k in range(tp_count):
            pack_ref[:, k * width : (k + 1) * width] = source[k][...]

    @pl.when(info[0] == 0)
    def _():
        run(other_ref, 0)
        pack(blocks)

    @pl.when(info[0] == 1)
    def _():
        run(own_ref, tokens)
        pack(early)


def slope_kernel(mixed_ref, scale_ref, out_ref):
    out_ref[...] = gelu_slope(mixed_ref[...]) * scale_ref[:, :1]


def turn_kernel(tp_count, x_count, info, *refs):
    first = refs[:tp_count]
    second = refs[tp_count : 2 * tp_count]
    other_ref = refs[2 * tp_count]
    outs = refs[2 * tp_count + 1 : 2 * tp_count + 1 + x_count]
    turned = refs[-1]
    tp_pos = info[2]
    x_pos = lax.rem(info[1], x_count)
    rows = turned.shape[2]
    width = first[0].shape[1]

    def put(blocks):
        for k in range(tp_count):
            source = lax.rem(tp_pos + tp_count - k, tp_count)
            both = jnp.concatenate(
                [blocks[k][...], other_ref[:, k * width : (k + 1) * width]], axis=0
            )
            flipped = both.T
            per = width // rows
            for i in range(per):
                place = source * (per // x_count) + i // x_count
                turned[i % x_count, place] = flipped[i * rows : (i + 1) * rows]

    @pl.when(info[0] == 0)
    def _():
        put(first)

    @pl.when(info[0] == 1)
    def _():
        put(second)

    for k in range(x_count):
        chunk = turned[lax.rem(x_pos + k, x_count)]
        outs[k][: chunk.shape[0] * rows] = chunk.reshape(-1, chunk.shape[2])


def delta_kernel(tp_count, info, *refs):
    back = refs[:tp_count]
    slope_ref, last_ref, keep_ref, send_ref = refs[tp_count:]
    grad = back[0][...].astype(F32)
    for ref in back[1:]:
        grad = grad + ref[...].astype(F32)
    grad = grad.astype(BF).astype(F32)
    delta = (grad * slope_ref[...]).astype(BF)

    @pl.when(info[0] == 0)
    def _():
        keep_ref[...] = delta
        send_ref[...] = last_ref[...]

    @pl.when(info[0] == 1)
    def _():
        keep_ref[...] = last_ref[...]
        send_ref[...] = delta


def join_kernel(a_ref, b_ref, *refs):
    out_ref, trio_ref = refs[-2:]
    for k in range(3):
        trio_ref[k] = refs[k][...]
    half = a_ref.shape[0]
    out_ref[:half] = a_ref[...]
    out_ref[half:] = b_ref[...]


def part_kernel(x_count, z_count, info, *refs):
    turned, deltas = refs[:x_count], refs[x_count : 2 * x_count]
    own_ref, plus_ref, minus_ref, far_ref, wide_ref, parts = refs[2 * x_count + 1 :]
    left = jnp.concatenate([t[...] for t in turned], axis=1)
    right = jnp.concatenate([d[...] for d in deltas], axis=0)
    part = jnp.dot(left, right, preferred_element_type=F32).astype(BF)
    parts[...] = part.reshape(parts.shape)
    z_pos = info[1] // x_count

    def chunk(k):
        return parts[lax.rem(z_pos + z_count + k, z_count)]

    width = far_ref.shape[1]
    split = plus_ref.shape[1] - 2 * width
    own_ref[...] = chunk(0)
    far_ref[...] = chunk(3)
    wide_ref[...] = chunk(-3)
    plus_ref[:, :width] = chunk(1)
    plus_ref[:, width : 2 * width] = chunk(-2)
    plus_ref[:, 2 * width :] = chunk(4)[:, :split]
    minus_ref[:, :width] = chunk(-1)
    minus_ref[:, width : 2 * width] = chunk(2)
    minus_ref[:, 2 * width :] = chunk(4)[:, split:]


def middle_kernel(plus_ref, minus_ref, far_ref, wide_ref, up_ref, down_ref):
    width = far_ref.shape[1]
    split = plus_ref.shape[1] - 2 * width
    up = far_ref[...].astype(F32) + minus_ref[:, width : 2 * width].astype(F32)
    down = wide_ref[...].astype(F32) + plus_ref[:, width : 2 * width].astype(F32)
    up_ref[:, :split] = (up[:, :split] + plus_ref[:, 2 * width :].astype(F32)).astype(BF)
    up_ref[:, split:] = up[:, split:].astype(BF)
    down_ref[:, :split] = down[:, :split].astype(BF)
    down_ref[:, split:] = (down[:, split:] + minus_ref[:, 2 * width :].astype(F32)).astype(BF)


def sum_kernel(own_ref, plus_ref, minus_ref, up_ref, down_ref, out_ref):
    width = own_ref.shape[1]
    total = own_ref[...].astype(F32) + plus_ref[:, :width].astype(F32)
    total = total + minus_ref[:, :width].astype(F32)
    out_ref[...] = total + up_ref[...].astype(F32) + down_ref[...].astype(F32)


def plan_kernel(x_count, z_count, info, wiring, _, plan, counts):
    x_pos = lax.rem(info[1], x_count)
    z_pos = info[1] // x_count
    for i in range(x_count * WCAP + WCAP):
        plan[i] = -1
    for i in range(x_count):
        counts[i] = 0
    for j in range(x_count * z_count):
        r = wiring[0, 0, j]

        @pl.when(r // x_count == z_pos)
        def _(j=j, r=r):
            column = lax.rem(r, x_count)
            slot = jnp.minimum(counts[column], WCAP - 1)
            counts[column] = slot + 1

            @pl.when(x_pos == j % x_count)
            def _():
                shift = lax.rem(column + x_count - x_pos, x_count)
                plan[shift * WCAP + slot] = lax.rem(z_pos + z_count - j // x_count, z_count)

            @pl.when(column == x_pos)
            def _():
                plan[x_count * WCAP + slot] = lax.rem(x_pos + x_count - j % x_count, x_count)


def route_kernel(x_count, z_count, plan, *refs):
    near, outs = refs[:3], refs[-x_count:]
    for k in range(x_count):
        for c in range(WCAP):
            steps = plan[k * WCAP + c]
            for m, (group, place) in enumerate(AWAY):

                @pl.when(steps == m)
                def _(k=k, c=c, group=group, place=place):
                    outs[k][c] = near[group][place]


def pick_kernel(x_count, info, plan, x1_ref, *refs):
    slots, send_ref = refs[:x_count], refs[-1]

    @pl.when(info[0] == 0)
    def _():
        for c in range(WCAP):
            steps = plan[x_count * WCAP + c]
            for k in range(x_count):

                @pl.when(steps == k)
                def _(c=c, k=k):
                    send_ref[c] = slots[k][c]

            @pl.when(steps < 0)
            def _(c=c):
                send_ref[c] = jnp.zeros_like(x1_ref)

    @pl.when(info[0] == 1)
    def _():
        send_ref[0] = x1_ref[...]
        for c in range(1, WCAP):
            send_ref[c] = jnp.zeros_like(x1_ref)


def acts_kernel(x_count, info, plan, x1_ref, come_ref, *refs):
    slots, (out_ref, blank, sems) = refs[:x_count], refs[x_count:]
    half = x1_ref.shape[0]

    def put(source, c, own):
        base = own * half
        place = out_ref.at[c, pl.ds(base, half), :]
        return pltpu.make_async_copy(source, place, sems.at[c * 2 + own])

    blank[...] = jnp.zeros_like(blank)

    @pl.when(info[0] == 0)
    def _():
        put(x1_ref, 0, 0).start()
        for c in range(1, WCAP):
            put(blank, c, 0).start()
        for c in range(WCAP):
            put(come_ref.at[c], c, 1).start()

    @pl.when(info[0] == 1)
    def _():
        for c in range(WCAP):
            put(come_ref.at[c], c, 0).start()
            steps = plan[x_count * WCAP + c]
            for k in range(x_count):

                @pl.when(steps == k)
                def _(c=c, k=k):
                    put(slots[k].at[c], c, 1).start()

            @pl.when(steps < 0)
            def _(c=c):
                put(blank, c, 1).start()

    for c in range(WCAP):
        for own in range(2):
            put(blank, c, own).wait()


def on_device(x_count, z_count, inputs, weights, wiring, lengths, targets):
    replicas = lax.axis_size("rep")
    tp_count = lax.axis_size("tp")
    section = lax.axis_index("section")
    rep = lax.axis_index("rep")
    tp = lax.axis_index("tp")
    info = jnp.stack([section, rep, tp]).astype(jnp.int32)
    _, _, tokens, width = inputs.shape
    half = tokens // 2
    weight = weights[0]
    feat = weight.shape[0]
    goal = targets.reshape(tokens, width)
    rows = feat // replicas
    loss_scale = 1.0 / math.sqrt(replicas * tokens)

    def swap(value, label):
        with jax.named_scope(label):
            return lax.ppermute(value, "section", [(0, 1), (1, 0)])

    def tp_move(value, k, label):
        pairs = [(y, (y + k) % tp_count) for y in range(tp_count)]
        with jax.named_scope(label):
            return lax.ppermute(value, "tp", pairs)

    def x_move(value, k, label):
        pairs = [
            (z * x_count + x, z * x_count + (x + k) % x_count)
            for z in range(z_count)
            for x in range(x_count)
        ]
        with jax.named_scope(label):
            return lax.ppermute(value, "rep", pairs)

    def z_move(value, k, label):
        pairs = [
            (z * x_count + x, ((z + k) % z_count) * x_count + x)
            for z in range(z_count)
            for x in range(x_count)
        ]
        with jax.named_scope(label):
            return lax.ppermute(value, "rep", pairs)

    def shape(*dims, dtype=BF):
        return jax.ShapeDtypeStruct(dims, dtype)

    flops = 2 * half * feat * width
    other_weight = swap(weight, "swap_weight")
    plan = pl.pallas_call(
        functools.partial(plan_kernel, x_count, z_count),
        out_shape=shape(x_count * WCAP + WCAP, dtype=jnp.int32),
        in_specs=[SM, SM, VM],
        out_specs=SM,
        scratch_shapes=[pltpu.SMEM((x_count,), jnp.int32)],
        name="plan",
        compiler_params=pltpu.CompilerParams(vmem_limit_bytes=VMEM_LIMIT),
    )(info, wiring, weight)
    x0 = lax.dynamic_slice(inputs.reshape(tokens, width), (section * half, 0), (half, width))
    first_blocks = [x0] + [tp_move(x0, k, "gather_x0") for k in range(1, tp_count)]
    x1, mixed, scale = call(
        functools.partial(first_kernel, tp_count, feat),
        (shape(half, width), shape(half, width, dtype=F32), shape(half, 128, dtype=F32)),
        [SM, SM] + [VM] * (tp_count + 2),
        "first",
        flops=flops,
        nbytes=2 * feat * width,
    )(info, plan, *first_blocks, weight, other_weight)
    slope = call(slope_kernel, shape(half, width, dtype=F32), [VM, VM], "slope")(mixed, scale)
    second_blocks = [x1] + [tp_move(x1, k, "gather_x1") for k in range(1, tp_count)]
    x2, delta1, packed, *back = call(
        functools.partial(second_kernel, tp_count, feat, loss_scale),
        (shape(half, width), shape(half, width), shape(half, feat))
        + (shape(half, width),) * tp_count,
        [SM, SM] + [VM] * (2 * tp_count + 4),
        "second",
        flops=2 * flops,
        nbytes=2 * feat * width,
    )(info, lengths, slope, *first_blocks, *second_blocks, weight, other_weight, goal)
    back_blocks = [back[0]] + [tp_move(back[k], tp_count - k, "sum_back") for k in range(1, tp_count)]
    other_pack = swap(packed, "swap_rows")
    turned = call(
        functools.partial(turn_kernel, tp_count, x_count),
        (shape(feat // x_count, tokens),) * x_count,
        [SM] + [VM] * (2 * tp_count + 1),
        "turn",
        scratch=[pltpu.VMEM((x_count, z_count, rows, tokens), BF)],
        flops=flops // 4,
        nbytes=2 * feat * tokens,
    )(info, *first_blocks, *second_blocks, other_pack)
    far = [x2, z_move(x2, 3, "route_far"), z_move(x2, z_count - 3, "route_far")]
    lefts = [turned[0]] + [x_move(turned[k], k, "spread_rows") for k in range(1, x_count)]
    keep, send = call(
        functools.partial(delta_kernel, tp_count),
        (shape(half, width), shape(half, width)),
        [SM] + [VM] * (tp_count + 2),
        "delta",
        flops=half * width,
        nbytes=8 * half * width,
    )(info, *back_blocks, slope, delta1)
    come = swap(send, "swap_delta")
    delta, trio = call(
        join_kernel,
        (shape(tokens, width), shape(3, half, width)),
        [VM] * (4 + x_count),
        "join",
    )(keep, come, *far, *lefts[1:])
    rights = [delta] + [x_move(delta, k, "gather_delta") for k in range(1, x_count)]
    near = [
        trio,
        z_move(trio, 1, "route_near"),
        z_move(trio, z_count - 1, "route_near"),
    ]
    pair = shape(WCAP, half, width)
    slots = call(
        functools.partial(route_kernel, x_count, z_count),
        (pair,) * x_count,
        [SM] + [VM] * 3,
        "route",
        nbytes=2 * z_count * half * width,
    )(plan, *near)
    chunk = shape(rows, width)
    split = -(-width // 256) * 128
    own, plus, minus, far_part, wide_part = call(
        functools.partial(part_kernel, x_count, z_count),
        (chunk, shape(rows, 2 * width + split), shape(rows, 3 * width - split), chunk, chunk),
        [SM] + [VM] * (2 * x_count + 1),
        "part",
        scratch=[pltpu.VMEM((z_count, rows, width), BF)],
        flops=2 * flops,
        nbytes=4 * feat * tokens,
    )(info, *lefts, *rights, slots[0])
    plus, minus = z_move(plus, 1, "part_near"), z_move(minus, z_count - 1, "part_near")
    up, down = call(middle_kernel, (chunk, chunk), [VM] * 4, "middle")(
        plus, minus, far_part, wide_part
    )
    up, down = z_move(up, 3, "part_far"), z_move(down, z_count - 3, "part_far")
    arrived = [slots[0]] + [x_move(slots[k], k, "route_x") for k in range(1, x_count)]
    sent = call(
        functools.partial(pick_kernel, x_count),
        pair,
        [SM, SM] + [VM] * (x_count + 1),
        "pick",
        flops=FILL,
        nbytes=2 * z_count * half * width,
    )(info, plan, x1, *arrived)
    grad_rows = call(sum_kernel, shape(rows, width, dtype=F32), [VM] * 5, "sum")(
        own, plus, minus, up, down
    )
    acts = pl.pallas_call(
        functools.partial(acts_kernel, x_count),
        out_shape=shape(WCAP, tokens, width),
        in_specs=[SM, SM] + [VM] * (x_count + 2),
        out_specs=pl.BlockSpec(memory_space=pl.ANY),
        scratch_shapes=[
            pltpu.VMEM((half, width), BF),
            pltpu.SemaphoreType.DMA((2 * WCAP,)),
        ],
        name="acts",
        compiler_params=pltpu.CompilerParams(vmem_limit_bytes=VMEM_LIMIT),
    )(info, plan, x1, swap(sent, "swap_acts"), *arrived)
    return (
        acts.reshape(1, 1, 1, WCAP, tokens, width),
        grad_rows.reshape(1, rows, width),
    )


def solution(mesh):
    in_specs = (
        P(None, "rep", None, "tp"),
        P("section", None, "tp"),
        P(),
        P(),
        P(None, "rep", None, "tp"),
    )
    out_specs = (P("section", None, "rep", None, None, "tp"), P("section", "rep", "tp"))
    x_count = 4
    z_count = mesh.shape["rep"] // x_count
    return jax.shard_map(
        functools.partial(on_device, x_count, z_count),
        mesh=mesh,
        in_specs=in_specs,
        out_specs=out_specs,
        check_vma=False,
    )
```
